32 devices in a mesh: feeder: 8 (over y, x, core), scen: 4 (over z).
Axes of the slice: x: 2, y: 2, z: 4, core: 2. Of those that a mesh axis runs over, the one named last changes fastest.
Arguments:
- anchor: bfloat16 [64, 24, 4096], P('scen', None, 'feeder'), may hold values from -6 to 6
- cost_lin: bfloat16 [64, 24, 4096], P('scen', None, 'feeder'), may hold values from -6 to 6
- dual: float32 [64, 24, 4096], P('scen', None, 'feeder'), may hold values from -4 to 4
- target: float32 [64, 24], P('scen'), may hold values from -4 to 4
- leaf_weight: float32 [64], P('scen'), may hold values from 1 to 10
- q_mat: bfloat16 [4096, 512], P('feeder'), may hold values from -0.25 to 0.25
- diag_gain: float32 [4096], P('feeder'), may hold values from 0.5 to 2
- block_mask: int32 [8, 4, 4], P('feeder'), may hold values from 0 to 1, as said below
- ancestor: int32 [24, 64], P(None, 'scen'), may hold values from 0 to 63, as said below
Outputs:
- setpoints: float32 [64, 24, 4096], P('scen', None, 'feeder')
- average: float32 [64, 24, 4096], P('scen', None, 'feeder')
- new_dual: float32 [64, 24, 4096], P('scen', None, 'feeder')
The draws below stay inside these ranges and needn't reach their ends.
Inputs may be any that keep to these rules, and one draw needn't show every extreme that they name: `block_mask`: every diagonal block is present; the share of present off-diagonal blocks differs from feeder to feeder. ancestor[t, s] is the first leaf of the section-t tree node that holds leaf s: the leaves of a node are consecutive, ancestor[0, s] = 0, and every section-t node lies inside one section-(t-1) node. Nodes may span several groups at any section.
All inputs are finite; a program needn't handle non-finite values.
Results may differ from the reference program's by a relative error of at most 0.0003.
Values sent between devices are 32-bit elements; how exact they have to be, the bound alone decides.
A program may use at most 64 MiB of HBM per device.

```python
import math
import jax
import jax.numpy as jnp
from jax import lax

NODES = 512
BLOCK = 128
SECTIONS = 24
PROX_ITERS = 8
NBLK = 4
FEEDERS = 8
SCEN = 64


def draw_block_mask(key, part):
    density = jax.random.randint(jax.random.fold_in(key, 11), (FEEDERS, 1, 1), 0, 4)
    rolls = jax.random.randint(jax.random.fold_in(key, 12), (FEEDERS, NBLK, NBLK), 0, 4)
    present = (rolls < density).astype(jnp.int32)
    diagonal = jnp.eye(NBLK, dtype=jnp.int32)[None, :, :]
    return jnp.maximum(present, diagonal)


def draw_ancestor(key, part):
    appear = jax.random.randint(jax.random.fold_in(key, 21), (SCEN,), 1, 2 * SECTIONS)
    leaf_ids = jnp.arange(SCEN, dtype=jnp.int32)
    appear = jnp.where(leaf_ids == SCEN - 1, SECTIONS - 1, appear)
    section_ids = jnp.arange(SECTIONS, dtype=jnp.int32)[:, None]
    starts = jnp.where((appear[None, :] <= section_ids) | (leaf_ids[None, :] == 0), leaf_ids[None, :], 0)
    return lax.cummax(starts, axis=1).astype(jnp.int32)


def block_levels(own_key, dims, pieces, smallest, high):
    def one(axis_at, shards_of):
        draws = jax.random.uniform(jax.random.fold_in(jax.random.fold_in(own_key, 6), axis_at), (shards_of,), jnp.float32, smallest / len(pieces), high / len(pieces))
        return jnp.repeat(jnp.exp(draws), dims[axis_at] // shards_of).reshape((-1,) + (1,) * (len(dims) - axis_at - 1))

    factor_of = one(*pieces[0])
    for cut in pieces[1:]:
        factor_of = factor_of * one(*cut)
    return factor_of


def scatter_about(own_key, shape, scale, limit, shards=(), held_as=jnp.bfloat16):
    factor_of = block_levels(own_key, shape, shards, -0.22, 0.18) if shards else 1.0
    result = jax.random.normal(own_key, shape, jnp.float32) * scale * factor_of
    return jnp.minimum(jnp.maximum(result, -limit), limit).astype(held_as)


def setup_inputs(seed: int = 0) -> dict:
    seeds = jax.random.split(jax.random.key(seed), 10)
    anchor = scatter_about(seeds[0], (SCEN, SECTIONS, FEEDERS * NODES), 1.0, 6.0, ((0, 4), (2, 8)))
    cost_lin = scatter_about(seeds[1], (SCEN, SECTIONS, FEEDERS * NODES), 1.0, 6.0, ((0, 4), (2, 8)))
    dual = scatter_about(seeds[2], (SCEN, SECTIONS, FEEDERS * NODES), 0.5, 4.0, ((0, 4), (2, 8)), jnp.float32)
    target = scatter_about(seeds[3], (SCEN, SECTIONS), 1.0, 4.0, ((0, 4),), jnp.float32)
    leaf_weight = jnp.clip(jnp.exp(math.log(10.0) - 2.3025851 * jax.random.uniform(seeds[4], (SCEN,), jnp.float32) ** block_levels(seeds[4], (SCEN,), ((0, 4),), -0.2, 0.2)), 1.0, 10.0)
    q_mat = scatter_about(seeds[5], (FEEDERS * NODES, NODES), NODES ** -0.5, 0.25, ((0, 8),))
    diag_gain = jnp.clip(jnp.exp(math.log(2.0) - 1.3862944 * jax.random.uniform(seeds[6], (FEEDERS * NODES,), jnp.float32) ** block_levels(seeds[6], (FEEDERS * NODES,), ((0, 8),), -0.2, 0.2)), 0.5, 2.0)
    block_mask = draw_block_mask(jax.random.fold_in(seeds[9], 71), 0)
    ancestor = draw_ancestor(jax.random.fold_in(seeds[9], 71), 0)
    return dict(anchor=anchor, cost_lin=cost_lin, dual=dual, target=target, leaf_weight=leaf_weight, q_mat=q_mat, diag_gain=diag_gain, block_mask=block_mask, ancestor=ancestor)


penalty = 1.0
step_size = 0.08
coupling = 4.0
power_limit = 2.0


def reference(anchor, cost_lin, dual, target, leaf_weight, q_mat, diag_gain, block_mask, ancestor):
    width_all = FEEDERS * NODES
    expand = jnp.repeat(jnp.repeat(block_mask, BLOCK, axis=1), BLOCK, axis=2)
    q_eff = q_mat.reshape(FEEDERS, NODES, NODES).astype(jnp.float32) * expand.astype(jnp.float32)
    start_pt = anchor.astype(jnp.float32)
    state = start_pt
    for sweep in range(PROX_ITERS):
        flat = state.reshape(SCEN * SECTIONS, FEEDERS, NODES).astype(jnp.bfloat16).astype(jnp.float32)
        image = jnp.einsum('rfn,fnm->rfm', flat, q_eff).reshape(SCEN, SECTIONS, width_all)
        head = jnp.sum(state, axis=2) / width_all
        grad = image + 2.0 * diag_gain * state + cost_lin.astype(jnp.float32) + dual
        grad = grad + penalty * (state - start_pt) + coupling * (head - target)[:, :, None]
        state = jnp.clip(state - step_size * grad, -power_limit, power_limit)
    weighted = leaf_weight[:, None, None] * state
    section_avgs = []
    for section in range(SECTIONS):
        owners = ancestor[section]
        sums = jax.ops.segment_sum(weighted[:, section, :], owners, num_segments=SCEN)
        weights = jax.ops.segment_sum(leaf_weight, owners, num_segments=SCEN)
        section_avgs.append(sums[owners] / weights[owners][:, None])
    average = jnp.stack(section_avgs, axis=1)
    new_dual = dual + penalty * (state - average)
    return state, average, new_dual
```

```python
import functools

import jax
import jax.numpy as jnp
from jax import lax
from jax.experimental import pallas as pl
from jax.experimental.pallas import tpu as pltpu
from jax.sharding import PartitionSpec as P

PROX_ITERS = 8

penalty = 1.0
step_size = 0.08
coupling = 4.0
power_limit = 2.0

LANES = 128
MESH = pl.DeviceIdType.MESH
F32 = jnp.float32
BF16 = jnp.bfloat16


def kernel(
    nf, ns,
    anchor_hbm, cost_hbm, dual_hbm, q_hbm, target_ref, weight_ref, diag_ref, mask_ref, anc_ref,
    x_hbm, avg_hbm, newdual_hbm,
    anchor_v, cost_v, dual_v, q_v, nat, fixed_nat, xt, pre, fixed_t, q_t, gain_t, head_col,
    x_out, avg_out, dual_out, total, same, inv, from_left, from_right,
    head_send, head_recv, note_send, note_recv, up_send, up_recv, down_send, down_recv, tail, front,
    in_sem, out_sem, head_ssem, head_rsem, note_ssem, note_rsem, up_ssem, up_rsem, down_ssem, down_rsem,
):
    leaves, sections, nodes = x_hbm.shape
    rows = leaves * sections
    lane_blocks = rows // LANES
    node_blocks = nodes // LANES
    mf, ms = lax.axis_index("feeder"), lax.axis_index("scen")

    barrier = pltpu.get_barrier_semaphore()
    for k in range(1, nf):
        pl.semaphore_signal(barrier, inc=1, device_id=(lax.rem(mf + k, nf), ms), device_id_type=MESH)
    for k in range(1, ns):
        pl.semaphore_signal(barrier, inc=1, device_id=(mf, lax.rem(ms + k, ns)), device_id_type=MESH)
    loads = [
        pltpu.make_async_copy(src, dst, in_sem.at[i])
        for i, (src, dst) in enumerate(
            ((anchor_hbm, anchor_v), (q_hbm, q_v), (cost_hbm, cost_v), (dual_hbm, dual_v))
        )
    ]
    for load in loads:
        load.start()

    def leaf_rows(leaf):
        return pl.ds(leaf * sections, sections)

    def lanes(block):
        return pl.ds(block * LANES, LANES)

    def send_heads(step):
        for k in range(1, nf):
            pltpu.make_async_remote_copy(
                src_ref=head_send.at[step],
                dst_ref=head_recv.at[step, k - 1],
                send_sem=head_ssem.at[step],
                recv_sem=head_rsem.at[step],
                device_id=(lax.rem(mf + k, nf), ms),
                device_id_type=MESH,
            ).start()

    def head_term(step):
        got = head_recv.at[step]
        pltpu.make_async_copy(got, got, head_rsem.at[step]).wait()
        pltpu.make_async_copy(got, got, head_ssem.at[step]).wait()
        whole = head_send[step]
        for k in range(nf - 1):
            whole = whole + head_recv[step, k]
        return whole * (step_size * coupling / (nf * nodes))

    def window():
        image = jnp.dot(q_t[...], xt[...].astype(BF16), preferred_element_type=F32)
        for b in range(lane_blocks):
            cols = slice(b * LANES, (b + 1) * LANES)
            pre[:, cols] = gain_t[...] * xt[:, cols] - step_size * image[:, cols] - fixed_t[:, cols]

    loads[0].wait()
    for leaf in range(leaves):
        nat[leaf_rows(leaf), :] = anchor_v[leaf].astype(F32)
    for b in range(lane_blocks):
        block = nat[lanes(b), :].T
        xt[:, lanes(b)] = block
        head_send[0, :, lanes(b)] = jnp.sum(block, axis=0, keepdims=True)
    pl.semaphore_wait(barrier, nf - 1 + ns - 1)
    send_heads(0)

    wide = (sections, LANES)
    ids = [jnp.broadcast_to(anc_ref[:, l : l + 1].astype(F32), wide) for l in range(leaves)]
    run_w = [jnp.full(wide, weight_ref[0], F32)]
    for l in range(1, leaves):
        link = (ids[l] == ids[l - 1]).astype(F32)
        same[l] = link
        run_w.append(link * run_w[-1] + weight_ref[l])
    total_w = [None] * leaves
    total_w[leaves - 1] = run_w[leaves - 1]
    for l in range(leaves - 2, -1, -1):
        total_w[l] = jnp.where(ids[l] == ids[l + 1], total_w[l + 1], run_w[l])
    for l in range(leaves):
        inv[l] = total_w[l]
    column = lax.broadcasted_iota(jnp.int32, wide, 1)
    note_send[...] = jnp.where(
        column == 0,
        run_w[leaves - 1],
        jnp.where(column == 1, ids[leaves - 1], jnp.where(column == 2, total_w[0], ids[0])),
    )
    for k in range(1, ns):
        pltpu.make_async_remote_copy(
            src_ref=note_send,
            dst_ref=note_recv.at[k - 1],
            send_sem=note_ssem,
            recv_sem=note_rsem,
            device_id=(mf, lax.rem(ms + k, ns)),
            device_id_type=MESH,
        ).start()

    loads[1].wait()
    for i in range(node_blocks):
        for j in range(node_blocks):
            keep = mask_ref[0, i, j].astype(F32)
            q_t[lanes(j), lanes(i)] = (q_v[lanes(i), lanes(j)].astype(F32) * keep).T.astype(BF16)
    gain_t[...] = 1.0 - step_size * (
        2.0 * jnp.broadcast_to(diag_ref[...], (LANES, nodes)).T + penalty
    )
    loads[2].wait()
    loads[3].wait()
    diagonal = lax.broadcasted_iota(jnp.int32, (sections, sections), 0) == lax.broadcasted_iota(
        jnp.int32, (sections, sections), 1
    )
    for l in range(leaves):
        goal = jnp.broadcast_to(target_ref[l : l + 1, :], (sections, sections))
        goal = jnp.sum(jnp.where(diagonal, goal, 0.0), axis=1, keepdims=True)
        fixed_nat[leaf_rows(l), :] = step_size * (
            cost_v[l].astype(F32) + dual_v[l] - penalty * nat[leaf_rows(l), :] - coupling * goal
        )
    for b in range(lane_blocks):
        fixed_t[:, lanes(b)] = fixed_nat[lanes(b), :].T
    window()

    def advance(step, carry):
        term = head_term(step - 1)
        part = jnp.zeros((8, rows), F32)
        for b in range(nodes // 64):
            some = slice(b * 64, (b + 1) * 64)
            new = jnp.clip(pre[some, :] - term, -power_limit, power_limit)
            xt[some, :] = new
            part = part + jnp.sum(new.reshape(8, 8, rows), axis=0)
        head_send[step] = jnp.sum(part, axis=0, keepdims=True)
        send_heads(step)
        window()
        return carry

    lax.fori_loop(1, 3, advance, 0)

    pltpu.make_async_copy(note_recv, note_recv, note_rsem).wait()
    pltpu.make_async_copy(note_recv, note_recv, note_ssem).wait()
    first_id = jnp.broadcast_to(anc_ref[:, 0:1].astype(F32), wide)
    last_id = jnp.broadcast_to(anc_ref[:, leaves - 1 : leaves].astype(F32), wide)
    start = (ms * leaves).astype(F32)
    goes_back = (first_id < start).astype(F32)
    spans = (last_id < start).astype(F32)
    left_w = jnp.zeros(wide, F32)
    right_w = jnp.zeros(wide, F32)
    for k in range(1, ns):
        note = note_recv[k - 1]
        earlier = jnp.where(ms >= k, 1.0, 0.0)
        left_w += earlier * jnp.where(note[:, 1:2] == first_id, note[:, 0:1], 0.0)
        right_w += (1.0 - earlier) * jnp.where(note[:, 3:4] == last_id, note[:, 2:3], 0.0)
    for l in range(leaves):
        own_id = jnp.broadcast_to(anc_ref[:, l : l + 1].astype(F32), wide)
        in_first = (own_id == first_id).astype(F32)
        in_last = (own_id == last_id).astype(F32)
        scale = 1.0 / (inv[l] + in_first * left_w + in_last * right_w)
        inv[l] = scale
        from_left[l] = in_first * goes_back * scale
        from_right[l] = in_last * scale

    lax.fori_loop(3, PROX_ITERS, advance, 0)

    for b in range(lane_blocks):
        nat[lanes(b), :] = pre[:, lanes(b)].T
    term = head_term(PROX_ITERS - 1)
    for b in range(lane_blocks):
        head_col[lanes(b), :] = jnp.broadcast_to(term[:, b * LANES : (b + 1) * LANES], (LANES, LANES)).T

    def up_copy(c):
        return pltpu.make_async_remote_copy(
            src_ref=up_send.at[c], dst_ref=up_recv.at[c],
            send_sem=up_ssem.at[c], recv_sem=up_rsem.at[c],
            device_id=(mf, lax.rem(ms + 1, ns)), device_id_type=MESH,
        )

    def down_copy(c):
        return pltpu.make_async_remote_copy(
            src_ref=down_send.at[c], dst_ref=down_recv.at[c],
            send_sem=down_ssem.at[c], recv_sem=down_rsem.at[c],
            device_id=(mf, lax.rem(ms + ns - 1, ns)), device_id_type=MESH,
        )

    at_bottom, at_top = ms == 0, ms == ns - 1
    for c in range(node_blocks):
        run = None
        for l in range(leaves):
            x = jnp.clip(nat[leaf_rows(l), lanes(c)] - head_col[leaf_rows(l), :], -power_limit, power_limit)
            x_out[l, :, lanes(c)] = x
            weighted = weight_ref[l] * x
            if l == 0:
                run = weighted
                opening = weighted
                in_first = goes_back
            else:
                run = weighted + same[l] * run
                in_first = in_first * same[l]
                opening = opening + in_first * weighted
            total[l, :, lanes(c)] = run
        opening = opening * goes_back
        tail[c] = run
        front[c] = opening

        @pl.when(at_bottom)
        def _():
            up_send[c] = run
            up_copy(c).start()

        @pl.when(at_top)
        def _():
            down_send[c] = opening
            down_copy(c).start()

    store_x = pltpu.make_async_copy(x_out, x_hbm, out_sem.at[0])
    store_x.start()

    for c in range(node_blocks):
        after = total[leaves - 1, :, lanes(c)]
        for l in range(leaves - 2, -1, -1):
            after = jnp.where(same[l + 1] > 0.5, after, total[l, :, lanes(c)])
            total[l, :, lanes(c)] = after

    def upward():
        for c in range(node_blocks):
            up_copy(c).wait_recv()

            @pl.when(jnp.logical_not(at_top))
            def _():
                up_send[c] = tail[c] + spans * up_recv[c]
                up_copy(c).start()

    def downward():
        for c in range(node_blocks):
            down_copy(c).wait_recv()

            @pl.when(jnp.logical_not(at_bottom))
            def _():
                down_send[c] = front[c] + spans * down_recv[c]
                down_copy(c).start()

    low = ms < ns // 2

    @pl.when(at_bottom)
    def _():
        up_recv[...] = jnp.zeros_like(up_recv)

    @pl.when(at_top)
    def _():
        down_recv[...] = jnp.zeros_like(down_recv)

    @pl.when(jnp.logical_and(low, jnp.logical_not(at_bottom)))
    def _():
        upward()

    @pl.when(jnp.logical_not(at_top))
    def _():
        downward()

    @pl.when(jnp.logical_not(low))
    def _():
        upward()

    stores = []
    for l in range(leaves):
        for c in range(node_blocks):
            average = (
                total[l, :, lanes(c)] * inv[l] + from_left[l] * up_recv[c] + from_right[l] * down_recv[c]
            )
            avg_out[l, :, lanes(c)] = average
            dual_out[l, :, lanes(c)] = dual_v[l, :, lanes(c)] + penalty * (x_out[l, :, lanes(c)] - average)
        if l % 4 == 3:
            done = pl.ds(l - 3, 4)
            for i, (src, dst) in enumerate(((avg_out, avg_hbm), (dual_out, newdual_hbm))):
                store = pltpu.make_async_copy(src.at[done], dst.at[done], out_sem.at[1 + 2 * (l // 4) + i])
                store.start()
                stores.append(store)
    for c in range(node_blocks):

        @pl.when(jnp.logical_not(at_top))
        def _():
            up_copy(c).wait_send()

        @pl.when(jnp.logical_not(at_bottom))
        def _():
            down_copy(c).wait_send()

    store_x.wait()
    for store in stores:
        store.wait()


def local(nf, ns, anchor, cost_lin, dual, target, leaf_weight, q_mat, diag_gain, block_mask, ancestor):
    leaves, sections, nodes = anchor.shape
    rows = leaves * sections
    blocks = nodes // LANES
    vmem, smem = pltpu.VMEM, pltpu.SMEM
    dma = pltpu.SemaphoreType.DMA
    cube = (leaves, sections, nodes)
    coef = (leaves, sections, LANES)
    piece = (blocks, sections, LANES)
    out = jax.ShapeDtypeStruct(cube, F32)
    far = pl.BlockSpec(memory_space=pl.ANY)
    near = pl.BlockSpec(memory_space=vmem)
    scalars = pl.BlockSpec(memory_space=smem)
    return pl.pallas_call(
        functools.partial(kernel, nf, ns),
        out_shape=(out, out, out),
        in_specs=[far, far, far, far, near, scalars, near, scalars, near],
        out_specs=(far, far, far),
        scratch_shapes=[
            vmem(cube, BF16), vmem(cube, BF16), vmem(cube, F32), vmem((nodes, nodes), BF16),
            vmem((rows, nodes), F32), vmem((rows, nodes), F32),
            vmem((nodes, rows), F32), vmem((nodes, rows), F32), vmem((nodes, rows), F32),
            vmem((nodes, nodes), BF16), vmem((nodes, LANES), F32), vmem((rows, LANES), F32),
            vmem(cube, F32), vmem(cube, F32), vmem(cube, F32), vmem(cube, F32),
            vmem(coef, F32), vmem(coef, F32), vmem(coef, F32), vmem(coef, F32),
            vmem((PROX_ITERS, 1, rows), F32), vmem((PROX_ITERS, nf - 1, 1, rows), F32),
            vmem((sections, LANES), F32), vmem((ns - 1, sections, LANES), F32),
            vmem(piece, F32), vmem(piece, F32), vmem(piece, F32), vmem(piece, F32),
            vmem(piece, F32), vmem(piece, F32),
            dma((4,)), dma((1 + leaves // 2,)), dma((PROX_ITERS,)), dma((PROX_ITERS,)), dma, dma,
            dma((blocks,)), dma((blocks,)), dma((blocks,)), dma((blocks,)),
        ],
        compiler_params=pltpu.CompilerParams(
            collective_id=0, has_side_effects=True, vmem_limit_bytes=56 * 1024 * 1024
        ),
        cost_estimate=pl.CostEstimate(
            flops=2 * PROX_ITERS * rows * nodes * nodes, bytes_accessed=24 * rows * nodes, transcendentals=0
        ),
    )(anchor, cost_lin, dual, q_mat, target, leaf_weight, diag_gain.reshape(1, nodes), block_mask, ancestor)


def solution(mesh):
    return jax.shard_map(
        functools.partial(local, mesh.shape["feeder"], mesh.shape["scen"]),
        mesh=mesh,
        in_specs=(
            P("scen", None, "feeder"),
            P("scen", None, "feeder"),
            P("scen", None, "feeder"),
            P("scen", None),
            P("scen"),
            P("feeder", None),
            P("feeder"),
            P("feeder", None, None),
            P(None, "scen"),
        ),
        out_specs=(P("scen", None, "feeder"), P("scen", None, "feeder"), P("scen", None, "feeder")),
        check_vma=False,
    )
```

```python
import functools

import jax
import jax.numpy as jnp
from jax import lax
from jax.experimental import pallas as pl
from jax.experimental.pallas import tpu as pltpu
from jax.sharding import PartitionSpec as P

PROX_ITERS = 8

penalty = 1.0
step_size = 0.08
coupling = 4.0
power_limit = 2.0

LANES = 128
MESH = pl.DeviceIdType.MESH
F32 = jnp.float32
BF16 = jnp.bfloat16


def kernel(
    nf, ns,
    anchor_hbm, cost_hbm, dual_hbm, q_hbm, target_ref, weight_ref, diag_ref, mask_ref, anc_ref,
    x_hbm, packed_ref,
    anchor_v, cost_v, dual_v, q_v, nat, fixed_nat, xt, pre, fixed_t, q_t, gain_t, head_col,
    x_out, small, total_w, same,
    head_send, head_recv, note_send, note_recv, up_send, up_recv, down_send, down_recv, tail, front,
    in_sem, out_sem, head_ssem, head_rsem, note_ssem, note_rsem, up_ssem, up_rsem, down_ssem, down_rsem,
):
    leaves, sections, nodes = x_hbm.shape
    rows = leaves * sections
    lane_blocks = rows // LANES
    node_blocks = nodes // LANES
    mf, ms = lax.axis_index("feeder"), lax.axis_index("scen")

    barrier = pltpu.get_barrier_semaphore()
    for k in range(1, nf):
        pl.semaphore_signal(barrier, inc=1, device_id=(lax.rem(mf + k, nf), ms), device_id_type=MESH)
    for k in range(1, ns):
        pl.semaphore_signal(barrier, inc=1, device_id=(mf, lax.rem(ms + k, ns)), device_id_type=MESH)
    loads = [
        pltpu.make_async_copy(src, dst, in_sem.at[i])
        for i, (src, dst) in enumerate(
            ((anchor_hbm, anchor_v), (q_hbm, q_v), (cost_hbm, cost_v), (dual_hbm, dual_v))
        )
    ]
    for load in loads:
        load.start()

    def leaf_rows(leaf):
        return pl.ds(leaf * sections, sections)

    def lanes(block):
        return pl.ds(block * LANES, LANES)

    def send_heads(step):
        for k in range(1, nf):
            pltpu.make_async_remote_copy(
                src_ref=head_send.at[step],
                dst_ref=head_recv.at[step, k - 1],
                send_sem=head_ssem.at[step],
                recv_sem=head_rsem.at[step],
                device_id=(lax.rem(mf + k, nf), ms),
                device_id_type=MESH,
            ).start()

    def head_term(step):
        got = head_recv.at[step]
        pltpu.make_async_copy(got, got, head_rsem.at[step]).wait()
        pltpu.make_async_copy(got, got, head_ssem.at[step]).wait()
        whole = head_send[step]
        for k in range(nf - 1):
            whole = whole + head_recv[step, k]
        return whole * (step_size * coupling / (nf * nodes))

    def window():
        image = jnp.dot(q_t[...], xt[...].astype(BF16), preferred_element_type=F32)
        for b in range(lane_blocks):
            cols = slice(b * LANES, (b + 1) * LANES)
            pre[:, cols] = gain_t[...] * xt[:, cols] - step_size * image[:, cols] - fixed_t[:, cols]

    loads[0].wait()
    for leaf in range(leaves):
        nat[leaf_rows(leaf), :] = anchor_v[leaf].astype(F32)
    for b in range(lane_blocks):
        block = nat[lanes(b), :].T
        xt[:, lanes(b)] = block
        head_send[0, :, lanes(b)] = jnp.sum(block, axis=0, keepdims=True)
    pl.semaphore_wait(barrier, nf - 1 + ns - 1)
    send_heads(0)

    wide = (sections, LANES)
    small[...] = jnp.zeros_like(small)
    small[0:leaves, 0:sections] = anc_ref[...].astype(F32)
    small[leaves : 2 * leaves, 0:sections] = target_ref[...]
    small[...] = small[...].T

    def leaf_id(l):
        return jnp.broadcast_to(small[0:sections, l : l + 1], wide)

    ids = [leaf_id(l) for l in range(leaves)]
    run_w = [jnp.full(wide, weight_ref[0], F32)]
    for l in range(1, leaves):
        link = (ids[l] == ids[l - 1]).astype(F32)
        same[l] = link
        run_w.append(link * run_w[-1] + weight_ref[l])
    own_w = run_w[leaves - 1]
    total_w[leaves - 1] = own_w
    for l in range(leaves - 2, -1, -1):
        own_w = jnp.where(ids[l] == ids[l + 1], own_w, run_w[l])
        total_w[l] = own_w
    column = lax.broadcasted_iota(jnp.int32, wide, 1)
    note_send[...] = jnp.where(
        column == 0,
        run_w[leaves - 1],
        jnp.where(column == 1, ids[leaves - 1], jnp.where(column == 2, own_w, ids[0])),
    )
    for k in range(1, ns):
        pltpu.make_async_remote_copy(
            src_ref=note_send,
            dst_ref=note_recv.at[k - 1],
            send_sem=note_ssem,
            recv_sem=note_rsem,
            device_id=(mf, lax.rem(ms + k, ns)),
            device_id_type=MESH,
        ).start()

    loads[1].wait()
    for i in range(node_blocks):
        for j in range(node_blocks):
            keep = mask_ref[0, i, j].astype(F32)
            q_t[lanes(j), lanes(i)] = (q_v[lanes(i), lanes(j)].astype(F32) * keep).T.astype(BF16)
    gain_t[...] = 1.0 - step_size * (
        2.0 * jnp.broadcast_to(diag_ref[...], (LANES, nodes)).T + penalty
    )
    loads[2].wait()
    loads[3].wait()
    for l in range(leaves):
        goal = small[0:sections, leaves + l : leaves + l + 1]
        fixed_nat[leaf_rows(l), :] = step_size * (
            cost_v[l].astype(F32) + dual_v[l] - penalty * nat[leaf_rows(l), :] - coupling * goal
        )
    for b in range(lane_blocks):
        fixed_t[:, lanes(b)] = fixed_nat[lanes(b), :].T
    window()

    def advance(step, carry):
        term = head_term(step - 1)
        part = jnp.zeros((8, rows), F32)
        for b in range(nodes // 64):
            some = slice(b * 64, (b + 1) * 64)
            new = jnp.clip(pre[some, :] - term, -power_limit, power_limit)
            xt[some, :] = new
            part = part + jnp.sum(new.reshape(8, 8, rows), axis=0)
        head_send[step] = jnp.sum(part, axis=0, keepdims=True)
        send_heads(step)
        window()
        return carry

    lax.fori_loop(1, 3, advance, 0)

    pltpu.make_async_copy(note_recv, note_recv, note_rsem).wait()
    pltpu.make_async_copy(note_recv, note_recv, note_ssem).wait()
    first_id = leaf_id(0)
    last_id = leaf_id(leaves - 1)
    start = (ms * leaves).astype(F32)
    goes_back = (first_id < start).astype(F32)
    spans = (last_id < start).astype(F32)
    left_w = jnp.zeros(wide, F32)
    right_w = jnp.zeros(wide, F32)
    for k in range(1, ns):
        note = note_recv[k - 1]
        earlier = jnp.where(ms >= k, 1.0, 0.0)
        left_w += earlier * jnp.where(note[:, 1:2] == first_id, note[:, 0:1], 0.0)
        right_w += (1.0 - earlier) * jnp.where(note[:, 3:4] == last_id, note[:, 2:3], 0.0)
    packed = jnp.zeros(wide, F32)
    for l in range(leaves):
        own_id = leaf_id(l)
        in_first = (own_id == first_id).astype(F32)
        in_last = (own_id == last_id).astype(F32)
        scale = 1.0 / (total_w[l] + in_first * left_w + in_last * right_w)
        packed = jnp.where(column == l, scale, packed)
        packed = jnp.where(column == leaves + l, in_first * goes_back * scale, packed)
        packed = jnp.where(column == 2 * leaves + l, in_last * scale, packed)
        if l > 0:
            packed = jnp.where(column == 3 * leaves + l, same[l], packed)
    packed_ref[2 * node_blocks] = packed

    lax.fori_loop(3, PROX_ITERS, advance, 0)

    for b in range(lane_blocks):
        nat[lanes(b), :] = pre[:, lanes(b)].T
    term = head_term(PROX_ITERS - 1)
    for b in range(lane_blocks):
        head_col[lanes(b), :] = jnp.broadcast_to(term[:, b * LANES : (b + 1) * LANES], (LANES, LANES)).T

    def up_copy(c):
        return pltpu.make_async_remote_copy(
            src_ref=up_send.at[c], dst_ref=up_recv.at[c],
            send_sem=up_ssem.at[c], recv_sem=up_rsem.at[c],
            device_id=(mf, lax.rem(ms + 1, ns)), device_id_type=MESH,
        )

    def down_copy(c):
        return pltpu.make_async_remote_copy(
            src_ref=down_send.at[c], dst_ref=down_recv.at[c],
            send_sem=down_ssem.at[c], recv_sem=down_rsem.at[c],
            device_id=(mf, lax.rem(ms + ns - 1, ns)), device_id_type=MESH,
        )

    at_bottom, at_top = ms == 0, ms == ns - 1
    for c in range(node_blocks):
        run = None
        for l in range(leaves):
            x = jnp.clip(nat[leaf_rows(l), lanes(c)] - head_col[leaf_rows(l), :], -power_limit, power_limit)
            x_out[l, :, lanes(c)] = x
            weighted = weight_ref[l] * x
            if l == 0:
                run = weighted
                opening = weighted
                in_first = goes_back
            else:
                run = weighted + same[l] * run
                in_first = in_first * same[l]
                opening = opening + in_first * weighted
        opening = opening * goes_back
        tail[c] = run
        front[c] = opening

        @pl.when(at_bottom)
        def _():
            up_send[c] = run
            up_copy(c).start()

        @pl.when(at_top)
        def _():
            down_send[c] = opening
            down_copy(c).start()

    store_x = pltpu.make_async_copy(x_out, x_hbm, out_sem.at[0])
    store_x.start()

    def upward():
        for c in range(node_blocks):
            up_copy(c).wait_recv()

            @pl.when(jnp.logical_not(at_top))
            def _():
                up_send[c] = tail[c] + spans * up_recv[c]
                up_copy(c).start()

    def downward():
        for c in range(node_blocks):
            down_copy(c).wait_recv()

            @pl.when(jnp.logical_not(at_bottom))
            def _():
                down_send[c] = front[c] + spans * down_recv[c]
                down_copy(c).start()

    low = ms < ns // 2

    @pl.when(at_bottom)
    def _():
        up_recv[...] = jnp.zeros_like(up_recv)

    @pl.when(at_top)
    def _():
        down_recv[...] = jnp.zeros_like(down_recv)

    @pl.when(jnp.logical_and(low, jnp.logical_not(at_bottom)))
    def _():
        upward()

    @pl.when(jnp.logical_not(at_top))
    def _():
        downward()

    @pl.when(jnp.logical_not(low))
    def _():
        upward()

    for c in range(node_blocks):
        packed_ref[c] = up_recv[c]
        packed_ref[node_blocks + c] = down_recv[c]
    for c in range(node_blocks):

        @pl.when(jnp.logical_not(at_top))
        def _():
            up_copy(c).wait_send()

        @pl.when(jnp.logical_not(at_bottom))
        def _():
            down_copy(c).wait_send()

    store_x.wait()


def finish(
    x_hbm, dual_hbm, packed_ref, weight_ref,
    xout_hbm, avg_hbm, newdual_hbm,
    x_v, dual_v, avg_v, new_v, coef, in_sem, out_sem,
):
    leaves, sections, nodes = x_hbm.shape
    node_blocks = nodes // LANES

    def lanes(block):
        return pl.ds(block * LANES, LANES)

    def load(c):
        return [
            pltpu.make_async_copy(src.at[:, :, lanes(c)], dst.at[:, :, lanes(c)], in_sem.at[2 * c + i])
            for i, (src, dst) in enumerate(((x_hbm, x_v), (dual_hbm, dual_v)))
        ]

    def store(c):
        return [
            pltpu.make_async_copy(src.at[:, :, lanes(c)], dst.at[:, :, lanes(c)], out_sem.at[3 * c + i])
            for i, (src, dst) in enumerate(((x_v, xout_hbm), (avg_v, avg_hbm), (new_v, newdual_hbm)))
        ]

    for c in range(node_blocks):
        for copy in load(c):
            copy.start()
    packed = packed_ref[2 * node_blocks]
    for i in range(4 * leaves):
        coef[i] = jnp.broadcast_to(packed[:, i : i + 1], (sections, LANES))
    scale, left, right, same = (lambda l, i=i: coef[i * leaves + l] for i in range(4))
    for c in range(node_blocks):
        from_x, from_dual = load(c)
        from_x.wait()
        run = weight_ref[0] * x_v[0, :, lanes(c)]
        avg_v[0, :, lanes(c)] = run
        for l in range(1, leaves):
            run = weight_ref[l] * x_v[l, :, lanes(c)] + same(l) * run
            avg_v[l, :, lanes(c)] = run
        from_dual.wait()
        total = run
        for l in range(leaves - 1, -1, -1):
            if l < leaves - 1:
                total = jnp.where(same(l + 1) > 0.5, total, avg_v[l, :, lanes(c)])
            average = total * scale(l) + left(l) * packed_ref[c] + right(l) * packed_ref[node_blocks + c]
            avg_v[l, :, lanes(c)] = average
            new_v[l, :, lanes(c)] = dual_v[l, :, lanes(c)] + penalty * (x_v[l, :, lanes(c)] - average)
        for copy in store(c):
            copy.start()
    for c in range(node_blocks):
        for copy in store(c):
            copy.wait()


def local(nf, ns, anchor, cost_lin, dual, target, leaf_weight, q_mat, diag_gain, block_mask, ancestor):
    leaves, sections, nodes = anchor.shape
    rows = leaves * sections
    blocks = nodes // LANES
    vmem, smem = pltpu.VMEM, pltpu.SMEM
    dma = pltpu.SemaphoreType.DMA
    cube = (leaves, sections, nodes)
    coef = (leaves, sections, LANES)
    piece = (blocks, sections, LANES)
    out = jax.ShapeDtypeStruct(cube, F32)
    far = pl.BlockSpec(memory_space=pl.ANY)
    near = pl.BlockSpec(memory_space=vmem)
    scalars = pl.BlockSpec(memory_space=smem)
    packed = jax.ShapeDtypeStruct((2 * blocks + 1, sections, LANES), F32)
    limit = 56 * 1024 * 1024
    state, parts = pl.pallas_call(
        functools.partial(kernel, nf, ns),
        out_shape=(out, packed),
        in_specs=[far, far, far, far, near, scalars, near, scalars, near],
        out_specs=(far, near),
        scratch_shapes=[
            vmem(cube, BF16), vmem(cube, BF16), vmem(cube, F32), vmem((nodes, nodes), BF16),
            vmem((rows, nodes), F32), vmem((rows, nodes), F32),
            vmem((nodes, rows), F32), vmem((nodes, rows), F32), vmem((nodes, rows), F32),
            vmem((nodes, nodes), BF16), vmem((nodes, LANES), F32), vmem((rows, LANES), F32),
            vmem(cube, F32), vmem((LANES, LANES), F32),
            vmem(coef, F32), vmem(coef, F32),
            vmem((PROX_ITERS, 1, rows), F32), vmem((PROX_ITERS, nf - 1, 1, rows), F32),
            vmem((sections, LANES), F32), vmem((ns - 1, sections, LANES), F32),
            vmem(piece, F32), vmem(piece, F32), vmem(piece, F32), vmem(piece, F32),
            vmem(piece, F32), vmem(piece, F32),
            dma((4,)), dma((1,)), dma((PROX_ITERS,)), dma((PROX_ITERS,)), dma, dma,
            dma((blocks,)), dma((blocks,)), dma((blocks,)), dma((blocks,)),
        ],
        compiler_params=pltpu.CompilerParams(
            collective_id=0, has_side_effects=True, vmem_limit_bytes=limit
        ),
        cost_estimate=pl.CostEstimate(
            flops=2 * PROX_ITERS * rows * nodes * nodes, bytes_accessed=12 * rows * nodes, transcendentals=0
        ),
    )(anchor, cost_lin, dual, q_mat, target, leaf_weight, diag_gain.reshape(1, nodes), block_mask, ancestor.T)
    return pl.pallas_call(
        finish,
        out_shape=(out, out, out),
        in_specs=[far, far, near, scalars],
        out_specs=(far, far, far),
        scratch_shapes=[
            vmem(cube, F32), vmem(cube, F32), vmem(cube, F32), vmem(cube, F32),
            vmem((4 * leaves, sections, LANES), F32), dma((2 * blocks,)), dma((3 * blocks,)),
        ],
        compiler_params=pltpu.CompilerParams(vmem_limit_bytes=limit),
        cost_estimate=pl.CostEstimate(flops=10 * rows * nodes, bytes_accessed=20 * rows * nodes, transcendentals=0),
    )(state, dual, parts, leaf_weight)


def solution(mesh):
    return jax.shard_map(
        functools.partial(local, mesh.shape["feeder"], mesh.shape["scen"]),
        mesh=mesh,
        in_specs=(
            P("scen", None, "feeder"),
            P("scen", None, "feeder"),
            P("scen", None, "feeder"),
            P("scen", None),
            P("scen"),
            P("feeder", None),
            P("feeder"),
            P("feeder", None, None),
            P(None, "scen"),
        ),
        out_specs=(P("scen", None, "feeder"), P("scen", None, "feeder"), P("scen", None, "feeder")),
        check_vma=False,
    )
```

```python
import functools

import jax
import jax.numpy as jnp
from jax import lax
from jax.experimental import pallas as pl
from jax.experimental.pallas import tpu as pltpu
from jax.sharding import PartitionSpec as P

PROX_ITERS = 8

penalty = 1.0
step_size = 0.08
coupling = 4.0
power_limit = 2.0

LANES = 128
MESH = pl.DeviceIdType.MESH
F32 = jnp.float32
BF16 = jnp.bfloat16


def kernel(
    nf, ns,
    anchor_hbm, cost_hbm, dual_hbm, q_hbm, target_ref, weight_ref, diag_ref, mask_ref, anc_ref,
    x_hbm, packed_ref,
    anchor_v, cost_v, dual_v, q_v, q_m, nat_b, nat, fixed_nat, xt, pre, fixed_t, q_t, gain_t, head_col,
    x_out, small, total_w, same,
    head_send, head_recv, note_send, note_recv, up_send, up_recv, down_send, down_recv, tail, front,
    in_sem, out_sem, head_ssem, head_rsem, note_ssem, note_rsem, up_ssem, up_rsem, down_ssem, down_rsem,
):
    leaves, sections, nodes = x_hbm.shape
    rows = leaves * sections
    lane_blocks = rows // LANES
    node_blocks = nodes // LANES
    mf, ms = lax.axis_index("feeder"), lax.axis_index("scen")

    def partner(k):
        other, bit = mf, 1
        while bit < nf:
            if k & bit:
                other = other + bit - 2 * bit * lax.rem(lax.div(mf, bit), 2)
            bit *= 2
        return other

    order = sorted(range(1, nf), key=lambda k: -bin(k >> 1).count("1"))

    barrier = pltpu.get_barrier_semaphore()
    for k in range(1, nf):
        pl.semaphore_signal(barrier, inc=1, device_id=(partner(k), ms), device_id_type=MESH)
    for k in range(1, ns):
        pl.semaphore_signal(barrier, inc=1, device_id=(mf, lax.rem(ms + k, ns)), device_id_type=MESH)
    loads = [
        pltpu.make_async_copy(src, dst, in_sem.at[i])
        for i, (src, dst) in enumerate(
            ((anchor_hbm, anchor_v), (q_hbm, q_v), (cost_hbm, cost_v), (dual_hbm, dual_v))
        )
    ]
    for load in loads:
        load.start()

    def leaf_rows(leaf):
        return pl.ds(leaf * sections, sections)

    def lanes(block):
        return pl.ds(block * LANES, LANES)

    def send_heads(step):
        for k in order:
            pltpu.make_async_remote_copy(
                src_ref=head_send.at[step],
                dst_ref=head_recv.at[step, k - 1],
                send_sem=head_ssem.at[step],
                recv_sem=head_rsem.at[step],
                device_id=(partner(k), ms),
                device_id_type=MESH,
            ).start()

    def head_term(step):
        got = head_recv.at[step]
        pltpu.make_async_copy(got, got, head_rsem.at[step]).wait()
        pltpu.make_async_copy(got, got, head_ssem.at[step]).wait()
        whole = head_send[step]
        for k in range(nf - 1):
            whole = whole + head_recv[step, k]
        return whole * (step_size * coupling / (nf * nodes))

    def window():
        image = jnp.dot(q_t[...], xt[...].astype(BF16), preferred_element_type=F32)
        for b in range(lane_blocks):
            cols = slice(b * LANES, (b + 1) * LANES)
            pre[:, cols] = gain_t[...] * xt[:, cols] - step_size * image[:, cols] - fixed_t[:, cols]

    loads[0].wait()
    for leaf in range(leaves):
        nat[leaf_rows(leaf), :] = anchor_v[leaf].astype(F32)
    nat_b[...] = nat[...].astype(BF16)
    ones = jnp.ones((8, nodes), BF16)
    sums = lax.dot_general(ones, nat_b[...], (((1,), (1,)), ((), ())), preferred_element_type=F32)
    head_send[0] = sums[0:1, :]
    pl.semaphore_wait(barrier, nf - 1 + ns - 1)
    send_heads(0)

    small[...] = jnp.zeros_like(small)
    small[0:leaves, 0:sections] = anc_ref[...].astype(F32)
    small[leaves : 2 * leaves, 0:sections] = target_ref[...]
    small[...] = small[...].T
    loads[1].wait()
    for i in range(node_blocks):
        for j in range(node_blocks):
            q_m[lanes(i), lanes(j)] = q_v[lanes(i), lanes(j)] * mask_ref[0, i, j].astype(F32).astype(BF16)
    loads[2].wait()
    loads[3].wait()
    image = jnp.dot(nat_b[...], q_m[...], preferred_element_type=F32)
    gain_row = 1.0 - step_size * (2.0 * diag_ref[...] + penalty)
    for l in range(leaves):
        goal = small[0:sections, leaves + l : leaves + l + 1]
        here = nat[leaf_rows(l), :]
        fixed = step_size * (cost_v[l].astype(F32) + dual_v[l] - penalty * here - coupling * goal)
        fixed_nat[leaf_rows(l), :] = fixed
        nat[leaf_rows(l), :] = (
            gain_row * here - step_size * image[l * sections : (l + 1) * sections, :] - fixed
        )
    for b in range(lane_blocks):
        pre[:, lanes(b)] = nat[lanes(b), :].T

    def update(step):
        term = head_term(step - 1)
        part = jnp.zeros((8, rows), F32)
        for b in range(nodes // 64):
            some = slice(b * 64, (b + 1) * 64)
            new = jnp.clip(pre[some, :] - term, -power_limit, power_limit)
            xt[some, :] = new
            part = part + jnp.sum(new.reshape(8, 8, rows), axis=0)
        head_send[step] = jnp.sum(part, axis=0, keepdims=True)
        send_heads(step)

    def advance(step, carry):
        update(step)
        window()
        return carry

    update(1)
    q_t[...] = q_m[...].T
    for b in range(lane_blocks):
        fixed_t[:, lanes(b)] = fixed_nat[lanes(b), :].T
    gain_t[...] = jnp.broadcast_to(gain_row, (LANES, nodes)).T
    window()

    advance(2, 0)

    wide = (sections, LANES)

    def leaf_id(l):
        return jnp.broadcast_to(small[0:sections, l : l + 1], wide)

    ids = [leaf_id(l) for l in range(leaves)]
    run_w = [jnp.full(wide, weight_ref[0], F32)]
    for l in range(1, leaves):
        link = (ids[l] == ids[l - 1]).astype(F32)
        same[l] = link
        run_w.append(link * run_w[-1] + weight_ref[l])
    own_w = run_w[leaves - 1]
    total_w[leaves - 1] = own_w
    for l in range(leaves - 2, -1, -1):
        own_w = jnp.where(ids[l] == ids[l + 1], own_w, run_w[l])
        total_w[l] = own_w
    column = lax.broadcasted_iota(jnp.int32, wide, 1)
    note_send[...] = jnp.where(
        column == 0,
        run_w[leaves - 1],
        jnp.where(column == 1, ids[leaves - 1], jnp.where(column == 2, own_w, ids[0])),
    )
    for k in range(1, ns):
        pltpu.make_async_remote_copy(
            src_ref=note_send,
            dst_ref=note_recv.at[k - 1],
            send_sem=note_ssem,
            recv_sem=note_rsem,
            device_id=(mf, lax.rem(ms + k, ns)),
            device_id_type=MESH,
        ).start()

    lax.fori_loop(3, 5, advance, 0)

    pltpu.make_async_copy(note_recv, note_recv, note_rsem).wait()
    pltpu.make_async_copy(note_recv, note_recv, note_ssem).wait()
    first_id = leaf_id(0)
    last_id = leaf_id(leaves - 1)
    start = (ms * leaves).astype(F32)
    goes_back = (first_id < start).astype(F32)
    spans = (last_id < start).astype(F32)
    left_w = jnp.zeros(wide, F32)
    right_w = jnp.zeros(wide, F32)
    for k in range(1, ns):
        note = note_recv[k - 1]
        earlier = jnp.where(ms >= k, 1.0, 0.0)
        left_w += earlier * jnp.where(note[:, 1:2] == first_id, note[:, 0:1], 0.0)
        right_w += (1.0 - earlier) * jnp.where(note[:, 3:4] == last_id, note[:, 2:3], 0.0)
    packed = jnp.zeros(wide, F32)
    for l in range(leaves):
        own_id = leaf_id(l)
        in_first = (own_id == first_id).astype(F32)
        in_last = (own_id == last_id).astype(F32)
        scale = 1.0 / (total_w[l] + in_first * left_w + in_last * right_w)
        packed = jnp.where(column == l, scale, packed)
        packed = jnp.where(column == leaves + l, in_first * goes_back * scale, packed)
        packed = jnp.where(column == 2 * leaves + l, in_last * scale, packed)
        if l > 0:
            packed = jnp.where(column == 3 * leaves + l, same[l], packed)
    packed_ref[2 * node_blocks] = packed

    lax.fori_loop(5, PROX_ITERS, advance, 0)

    for b in range(lane_blocks):
        nat[lanes(b), :] = pre[:, lanes(b)].T
    term = head_term(PROX_ITERS - 1)
    for b in range(lane_blocks):
        head_col[lanes(b), :] = jnp.broadcast_to(term[:, b * LANES : (b + 1) * LANES], (LANES, LANES)).T

    def up_copy(c):
        return pltpu.make_async_remote_copy(
            src_ref=up_send.at[c], dst_ref=up_recv.at[c],
            send_sem=up_ssem.at[c], recv_sem=up_rsem.at[c],
            device_id=(mf, lax.rem(ms + 1, ns)), device_id_type=MESH,
        )

    def down_copy(c):
        return pltpu.make_async_remote_copy(
            src_ref=down_send.at[c], dst_ref=down_recv.at[c],
            send_sem=down_ssem.at[c], recv_sem=down_rsem.at[c],
            device_id=(mf, lax.rem(ms + ns - 1, ns)), device_id_type=MESH,
        )

    at_bottom, at_top = ms == 0, ms == ns - 1
    for c in range(node_blocks):
        run = None
        for l in range(leaves):
            x = jnp.clip(nat[leaf_rows(l), lanes(c)] - head_col[leaf_rows(l), :], -power_limit, power_limit)
            x_out[l, :, lanes(c)] = x
            weighted = weight_ref[l] * x
            if l == 0:
                run = weighted
                opening = weighted
                in_first = goes_back
            else:
                run = weighted + same[l] * run
                in_first = in_first * same[l]
                opening = opening + in_first * weighted
        opening = opening * goes_back
        tail[c] = run
        front[c] = opening

        @pl.when(at_bottom)
        def _():
            up_send[c] = run
            up_copy(c).start()

        @pl.when(at_top)
        def _():
            down_send[c] = opening
            down_copy(c).start()

    store_x = pltpu.make_async_copy(x_out, x_hbm, out_sem.at[0])
    store_x.start()

    def upward():
        for c in range(node_blocks):
            up_copy(c).wait_recv()

            @pl.when(jnp.logical_not(at_top))
            def _():
                up_send[c] = tail[c] + spans * up_recv[c]
                up_copy(c).start()

    def downward():
        for c in range(node_blocks):
            down_copy(c).wait_recv()

            @pl.when(jnp.logical_not(at_bottom))
            def _():
                down_send[c] = front[c] + spans * down_recv[c]
                down_copy(c).start()

    low = ms < ns // 2

    @pl.when(at_bottom)
    def _():
        up_recv[...] = jnp.zeros_like(up_recv)

    @pl.when(at_top)
    def _():
        down_recv[...] = jnp.zeros_like(down_recv)

    @pl.when(jnp.logical_and(low, jnp.logical_not(at_bottom)))
    def _():
        upward()

    @pl.when(jnp.logical_not(at_top))
    def _():
        downward()

    @pl.when(jnp.logical_not(low))
    def _():
        upward()

    for c in range(node_blocks):
        packed_ref[c] = up_recv[c]
        packed_ref[node_blocks + c] = down_recv[c]
    for c in range(node_blocks):

        @pl.when(jnp.logical_not(at_top))
        def _():
            up_copy(c).wait_send()

        @pl.when(jnp.logical_not(at_bottom))
        def _():
            down_copy(c).wait_send()

    store_x.wait()


def finish(
    x_hbm, dual_hbm, packed_ref, weight_ref,
    xout_hbm, avg_hbm, newdual_hbm,
    x_v, dual_v, avg_v, new_v, coef, in_sem, out_sem,
):
    leaves, sections, nodes = x_hbm.shape
    node_blocks = nodes // LANES

    def lanes(block):
        return pl.ds(block * LANES, LANES)

    def load(c):
        return [
            pltpu.make_async_copy(src.at[:, :, lanes(c)], dst.at[:, :, lanes(c)], in_sem.at[2 * c + i])
            for i, (src, dst) in enumerate(((x_hbm, x_v), (dual_hbm, dual_v)))
        ]

    def store(c):
        return [
            pltpu.make_async_copy(src.at[:, :, lanes(c)], dst.at[:, :, lanes(c)], out_sem.at[3 * c + i])
            for i, (src, dst) in enumerate(((x_v, xout_hbm), (avg_v, avg_hbm), (new_v, newdual_hbm)))
        ]

    for c in range(node_blocks):
        for copy in load(c):
            copy.start()
    packed = packed_ref[2 * node_blocks]
    for i in range(4 * leaves):
        coef[i] = jnp.broadcast_to(packed[:, i : i + 1], (sections, LANES))
    scale, left, right, same = (lambda l, i=i: coef[i * leaves + l] for i in range(4))
    for c in range(node_blocks):
        from_x, from_dual = load(c)
        from_x.wait()
        run = weight_ref[0] * x_v[0, :, lanes(c)]
        avg_v[0, :, lanes(c)] = run
        for l in range(1, leaves):
            run = weight_ref[l] * x_v[l, :, lanes(c)] + same(l) * run
            avg_v[l, :, lanes(c)] = run
        from_dual.wait()
        total = run
        for l in range(leaves - 1, -1, -1):
            if l < leaves - 1:
                total = jnp.where(same(l + 1) > 0.5, total, avg_v[l, :, lanes(c)])
            average = total * scale(l) + left(l) * packed_ref[c] + right(l) * packed_ref[node_blocks + c]
            avg_v[l, :, lanes(c)] = average
            new_v[l, :, lanes(c)] = dual_v[l, :, lanes(c)] + penalty * (x_v[l, :, lanes(c)] - average)
        for copy in store(c):
            copy.start()
    for c in range(node_blocks):
        for copy in store(c):
            copy.wait()


def local(nf, ns, anchor, cost_lin, dual, target, leaf_weight, q_mat, diag_gain, block_mask, ancestor):
    leaves, sections, nodes = anchor.shape
    rows = leaves * sections
    blocks = nodes // LANES
    vmem, smem = pltpu.VMEM, pltpu.SMEM
    dma = pltpu.SemaphoreType.DMA
    cube = (leaves, sections, nodes)
    coef = (leaves, sections, LANES)
    piece = (blocks, sections, LANES)
    out = jax.ShapeDtypeStruct(cube, F32)
    far = pl.BlockSpec(memory_space=pl.ANY)
    near = pl.BlockSpec(memory_space=vmem)
    scalars = pl.BlockSpec(memory_space=smem)
    packed = jax.ShapeDtypeStruct((2 * blocks + 1, sections, LANES), F32)
    limit = 56 * 1024 * 1024
    state, parts = pl.pallas_call(
        functools.partial(kernel, nf, ns),
        out_shape=(out, packed),
        in_specs=[far, far, far, far, near, scalars, near, scalars, near],
        out_specs=(far, near),
        scratch_shapes=[
            vmem(cube, BF16), vmem(cube, BF16), vmem(cube, F32), vmem((nodes, nodes), BF16),
            vmem((nodes, nodes), BF16), vmem((rows, nodes), BF16), vmem((rows, nodes), F32), vmem((rows, nodes), F32),
            vmem((nodes, rows), F32), vmem((nodes, rows), F32), vmem((nodes, rows), F32),
            vmem((nodes, nodes), BF16), vmem((nodes, LANES), F32), vmem((rows, LANES), F32),
            vmem(cube, F32), vmem((LANES, LANES), F32),
            vmem(coef, F32), vmem(coef, F32),
            vmem((PROX_ITERS, 1, rows), F32), vmem((PROX_ITERS, nf - 1, 1, rows), F32),
            vmem((sections, LANES), F32), vmem((ns - 1, sections, LANES), F32),
            vmem(piece, F32), vmem(piece, F32), vmem(piece, F32), vmem(piece, F32),
            vmem(piece, F32), vmem(piece, F32),
            dma((4,)), dma((1,)), dma((PROX_ITERS,)), dma((PROX_ITERS,)), dma, dma,
            dma((blocks,)), dma((blocks,)), dma((blocks,)), dma((blocks,)),
        ],
        compiler_params=pltpu.CompilerParams(
            collective_id=0, has_side_effects=True, vmem_limit_bytes=limit
        ),
        cost_estimate=pl.CostEstimate(
            flops=2 * PROX_ITERS * rows * nodes * nodes, bytes_accessed=12 * rows * nodes, transcendentals=0
        ),
    )(anchor, cost_lin, dual, q_mat, target, leaf_weight, diag_gain.reshape(1, nodes), block_mask, ancestor.T)
    return pl.pallas_call(
        finish,
        out_shape=(out, out, out),
        in_specs=[far, far, near, scalars],
        out_specs=(far, far, far),
        scratch_shapes=[
            vmem(cube, F32), vmem(cube, F32), vmem(cube, F32), vmem(cube, F32),
            vmem((4 * leaves, sections, LANES), F32), dma((2 * blocks,)), dma((3 * blocks,)),
        ],
        compiler_params=pltpu.CompilerParams(vmem_limit_bytes=limit),
        cost_estimate=pl.CostEstimate(flops=10 * rows * nodes, bytes_accessed=20 * rows * nodes, transcendentals=0),
    )(state, dual, parts, leaf_weight)


def solution(mesh):
    return jax.shard_map(
        functools.partial(local, mesh.shape["feeder"], mesh.shape["scen"]),
        mesh=mesh,
        in_specs=(
            P("scen", None, "feeder"),
            P("scen", None, "feeder"),
            P("scen", None, "feeder"),
            P("scen", None),
            P("scen"),
            P("feeder", None),
            P("feeder"),
            P("feeder", None, None),
            P(None, "scen"),
        ),
        out_specs=(P("scen", None, "feeder"), P("scen", None, "feeder"), P("scen", None, "feeder")),
        check_vma=False,
    )
```

```python
import functools

import jax
import jax.numpy as jnp
from jax import lax
from jax.experimental import pallas as pl
from jax.experimental.pallas import tpu as pltpu
from jax.sharding import PartitionSpec as P

PROX_ITERS = 8

penalty = 1.0
step_size = 0.08
coupling = 4.0
power_limit = 2.0

LANES = 128
MESH = pl.DeviceIdType.MESH
F32 = jnp.float32
BF16 = jnp.bfloat16


def kernel(
    nf, ns,
    anchor_hbm, cost_hbm, dual_hbm, q_hbm, target_ref, weight_ref, diag_ref, mask_ref, anc_ref,
    x_hbm, own_hbm, packed_ref,
    anchor_v, cost_v, dual_v, q_v, q_m, nat_b, nat, fixed_nat, xt, pre, fixed_t, q_t, gain_t, head_col,
    x_out, own_out, small, total_w, same,
    head_send, head_recv, note_send, note_recv, up_send, up_recv, down_send, down_recv, tail, front,
    in_sem, out_sem, head_ssem, head_rsem, note_ssem, note_rsem, up_ssem, up_rsem, down_ssem, down_rsem,
):
    leaves, sections, nodes = x_hbm.shape
    rows = leaves * sections
    lane_blocks = rows // LANES
    node_blocks = nodes // LANES
    mf, ms = lax.axis_index("feeder"), lax.axis_index("scen")

    def partner(k):
        other, bit = mf, 1
        while bit < nf:
            if k & bit:
                other = other + bit - 2 * bit * lax.rem(lax.div(mf, bit), 2)
            bit *= 2
        return other

    order = sorted(range(1, nf), key=lambda k: -bin(k >> 1).count("1"))

    barrier = pltpu.get_barrier_semaphore()
    for k in range(1, nf):
        pl.semaphore_signal(barrier, inc=1, device_id=(partner(k), ms), device_id_type=MESH)
    for k in range(1, ns):
        pl.semaphore_signal(barrier, inc=1, device_id=(mf, lax.rem(ms + k, ns)), device_id_type=MESH)
    loads = [
        pltpu.make_async_copy(src, dst, in_sem.at[i])
        for i, (src, dst) in enumerate(
            ((anchor_hbm, anchor_v), (q_hbm, q_v), (cost_hbm, cost_v), (dual_hbm, dual_v))
        )
    ]
    for load in loads:
        load.start()

    def leaf_rows(leaf):
        return pl.ds(leaf * sections, sections)

    def lanes(block):
        return pl.ds(block * LANES, LANES)

    def send_heads(step):
        for k in order:
            pltpu.make_async_remote_copy(
                src_ref=head_send.at[step],
                dst_ref=head_recv.at[step, k - 1],
                send_sem=head_ssem.at[step],
                recv_sem=head_rsem.at[step],
                device_id=(partner(k), ms),
                device_id_type=MESH,
            ).start()

    def head_term(step):
        got = head_recv.at[step]
        pltpu.make_async_copy(got, got, head_rsem.at[step]).wait()
        whole = head_send[step]
        for k in range(nf - 1):
            whole = whole + head_recv[step, k]
        return whole * (step_size * coupling / (nf * nodes))

    def window():
        image = jnp.dot(q_t[...], xt[...].astype(BF16), preferred_element_type=F32)
        for b in range(lane_blocks):
            cols = slice(b * LANES, (b + 1) * LANES)
            pre[:, cols] = gain_t[...] * xt[:, cols] - step_size * image[:, cols] - fixed_t[:, cols]

    loads[0].wait()
    for leaf in range(leaves):
        nat[leaf_rows(leaf), :] = anchor_v[leaf].astype(F32)
    nat_b[...] = nat[...].astype(BF16)
    ones = jnp.ones((8, nodes), BF16)
    sums = lax.dot_general(ones, nat_b[...], (((1,), (1,)), ((), ())), preferred_element_type=F32)
    head_send[0] = sums[0:1, :]
    pl.semaphore_wait(barrier, nf - 1 + ns - 1)
    send_heads(0)

    small[...] = jnp.zeros_like(small)
    small[0:leaves, 0:sections] = anc_ref[...].astype(F32)
    small[leaves : 2 * leaves, 0:sections] = target_ref[...]
    small[...] = small[...].T
    loads[1].wait()
    for i in range(node_blocks):
        for j in range(node_blocks):
            q_m[lanes(i), lanes(j)] = q_v[lanes(i), lanes(j)] * mask_ref[0, i, j].astype(F32).astype(BF16)
    loads[2].wait()
    loads[3].wait()
    image = jnp.dot(nat_b[...], q_m[...], preferred_element_type=F32)
    gain_row = 1.0 - step_size * (2.0 * diag_ref[...] + penalty)
    for l in range(leaves):
        goal = small[0:sections, leaves + l : leaves + l + 1]
        here = nat[leaf_rows(l), :]
        fixed = step_size * (cost_v[l].astype(F32) + dual_v[l] - penalty * here - coupling * goal)
        fixed_nat[leaf_rows(l), :] = fixed
        nat[leaf_rows(l), :] = (
            gain_row * here - step_size * image[l * sections : (l + 1) * sections, :] - fixed
        )
    for b in range(lane_blocks):
        pre[:, lanes(b)] = nat[lanes(b), :].T

    def update(step):
        term = head_term(step - 1)
        part = jnp.zeros((8, rows), F32)
        for b in range(nodes // 64):
            some = slice(b * 64, (b + 1) * 64)
            new = jnp.clip(pre[some, :] - term, -power_limit, power_limit)
            xt[some, :] = new
            part = part + jnp.sum(new.reshape(8, 8, rows), axis=0)
        head_send[step] = jnp.sum(part, axis=0, keepdims=True)
        send_heads(step)

    def advance(step, carry):
        update(step)
        window()
        return carry

    update(1)
    q_t[...] = q_m[...].T
    for b in range(lane_blocks):
        fixed_t[:, lanes(b)] = fixed_nat[lanes(b), :].T
    gain_t[...] = jnp.broadcast_to(gain_row, (LANES, nodes)).T
    window()

    advance(2, 0)

    wide = (sections, LANES)

    def leaf_id(l):
        return jnp.broadcast_to(small[0:sections, l : l + 1], wide)

    ids = [leaf_id(l) for l in range(leaves)]
    run_w = [jnp.full(wide, weight_ref[0], F32)]
    for l in range(1, leaves):
        link = (ids[l] == ids[l - 1]).astype(F32)
        same[l] = link
        run_w.append(link * run_w[-1] + weight_ref[l])
    own_w = run_w[leaves - 1]
    total_w[leaves - 1] = own_w
    for l in range(leaves - 2, -1, -1):
        own_w = jnp.where(ids[l] == ids[l + 1], own_w, run_w[l])
        total_w[l] = own_w
    column = lax.broadcasted_iota(jnp.int32, wide, 1)
    note_send[...] = jnp.where(
        column == 0,
        run_w[leaves - 1],
        jnp.where(column == 1, ids[leaves - 1], jnp.where(column == 2, own_w, ids[0])),
    )
    for k in range(1, ns):
        pltpu.make_async_remote_copy(
            src_ref=note_send,
            dst_ref=note_recv.at[k - 1],
            send_sem=note_ssem,
            recv_sem=note_rsem,
            device_id=(mf, lax.rem(ms + k, ns)),
            device_id_type=MESH,
        ).start()

    lax.fori_loop(3, 5, advance, 0)

    pltpu.make_async_copy(note_recv, note_recv, note_rsem).wait()
    pltpu.make_async_copy(note_recv, note_recv, note_ssem).wait()
    first_id = leaf_id(0)
    last_id = leaf_id(leaves - 1)
    start = (ms * leaves).astype(F32)
    goes_back = (first_id < start).astype(F32)
    spans = (last_id < start).astype(F32)
    left_w = jnp.zeros(wide, F32)
    right_w = jnp.zeros(wide, F32)
    for k in range(1, ns):
        note = note_recv[k - 1]
        earlier = jnp.where(ms >= k, 1.0, 0.0)
        left_w += earlier * jnp.where(note[:, 1:2] == first_id, note[:, 0:1], 0.0)
        right_w += (1.0 - earlier) * jnp.where(note[:, 3:4] == last_id, note[:, 2:3], 0.0)
    packed = jnp.zeros(wide, F32)
    for l in range(leaves):
        own_id = leaf_id(l)
        in_first = (own_id == first_id).astype(F32)
        in_last = (own_id == last_id).astype(F32)
        scale = 1.0 / (total_w[l] + in_first * left_w + in_last * right_w)
        total_w[l] = scale
        packed = jnp.where(column == l, in_first * goes_back * scale, packed)
        packed = jnp.where(column == leaves + l, in_last * scale, packed)
    packed_ref[2 * node_blocks] = packed

    lax.fori_loop(5, PROX_ITERS, advance, 0)

    for b in range(lane_blocks):
        nat[lanes(b), :] = pre[:, lanes(b)].T
    term = head_term(PROX_ITERS - 1)
    for b in range(lane_blocks):
        head_col[lanes(b), :] = jnp.broadcast_to(term[:, b * LANES : (b + 1) * LANES], (LANES, LANES)).T

    def up_copy(c):
        return pltpu.make_async_remote_copy(
            src_ref=up_send.at[c], dst_ref=up_recv.at[c],
            send_sem=up_ssem.at[c], recv_sem=up_rsem.at[c],
            device_id=(mf, lax.rem(ms + 1, ns)), device_id_type=MESH,
        )

    def down_copy(c):
        return pltpu.make_async_remote_copy(
            src_ref=down_send.at[c], dst_ref=down_recv.at[c],
            send_sem=down_ssem.at[c], recv_sem=down_rsem.at[c],
            device_id=(mf, lax.rem(ms + ns - 1, ns)), device_id_type=MESH,
        )

    at_bottom, at_top = ms == 0, ms == ns - 1
    for c in range(node_blocks):
        run = None
        for l in range(leaves):
            x = jnp.clip(nat[leaf_rows(l), lanes(c)] - head_col[leaf_rows(l), :], -power_limit, power_limit)
            x_out[l, :, lanes(c)] = x
            weighted = weight_ref[l] * x
            if l == 0:
                run = weighted
                opening = weighted
                in_first = goes_back
            else:
                run = weighted + same[l] * run
                in_first = in_first * same[l]
                opening = opening + in_first * weighted
            own_out[l, :, lanes(c)] = run
        opening = opening * goes_back
        tail[c] = run
        front[c] = opening

        @pl.when(at_bottom)
        def _():
            up_send[c] = run
            up_copy(c).start()

        @pl.when(at_top)
        def _():
            down_send[c] = opening
            down_copy(c).start()

    store_x = pltpu.make_async_copy(x_out, x_hbm, out_sem.at[0])
    store_x.start()
    for c in range(node_blocks):
        run = tail[c]
        for l in range(leaves - 1, -1, -1):
            if l < leaves - 1:
                run = jnp.where(same[l + 1] > 0.5, run, own_out[l, :, lanes(c)])
            own_out[l, :, lanes(c)] = run * total_w[l]
    store_own = pltpu.make_async_copy(own_out, own_hbm, out_sem.at[1])
    store_own.start()

    def upward():
        for c in range(node_blocks):
            up_copy(c).wait_recv()

            @pl.when(jnp.logical_not(at_top))
            def _():
                up_send[c] = tail[c] + spans * up_recv[c]
                up_copy(c).start()

    def downward():
        for c in range(node_blocks):
            down_copy(c).wait_recv()

            @pl.when(jnp.logical_not(at_bottom))
            def _():
                down_send[c] = front[c] + spans * down_recv[c]
                down_copy(c).start()

    low = ms < ns // 2

    @pl.when(at_bottom)
    def _():
        up_recv[...] = jnp.zeros_like(up_recv)

    @pl.when(at_top)
    def _():
        down_recv[...] = jnp.zeros_like(down_recv)

    @pl.when(jnp.logical_and(low, jnp.logical_not(at_bottom)))
    def _():
        upward()

    @pl.when(jnp.logical_not(at_top))
    def _():
        downward()

    @pl.when(jnp.logical_not(low))
    def _():
        upward()

    for c in range(node_blocks):
        packed_ref[c] = up_recv[c]
        packed_ref[node_blocks + c] = down_recv[c]
    for c in range(node_blocks):

        @pl.when(jnp.logical_not(at_top))
        def _():
            up_copy(c).wait_send()

        @pl.when(jnp.logical_not(at_bottom))
        def _():
            down_copy(c).wait_send()

    for step in range(PROX_ITERS):
        pltpu.make_async_copy(head_recv.at[step], head_recv.at[step], head_ssem.at[step]).wait()
    store_x.wait()
    store_own.wait()


def finish(
    x_hbm, own_hbm, dual_hbm, packed_ref,
    xout_hbm, avg_hbm, newdual_hbm,
    x_v, own_v, dual_v, coef, in_sem, out_sem,
):
    leaves, sections, nodes = x_hbm.shape
    node_blocks = nodes // LANES
    group = 4
    groups = leaves // group

    def moves(g, pairs, sem):
        some = pl.ds(g * group, group)
        return [
            pltpu.make_async_copy(src.at[some], dst.at[some], sem.at[3 * g + i])
            for i, (src, dst) in enumerate(pairs)
        ]

    def load(g):
        return moves(g, ((x_hbm, x_v), (own_hbm, own_v), (dual_hbm, dual_v)), in_sem)

    def store(g):
        return moves(g, ((x_v, xout_hbm), (own_v, avg_hbm), (dual_v, newdual_hbm)), out_sem)

    for g in range(groups):
        for copy in load(g):
            copy.start()
    packed = packed_ref[2 * node_blocks]
    for i in range(2 * leaves):
        coef[i] = jnp.broadcast_to(packed[:, i : i + 1], (sections, LANES))
    for g in range(groups):
        for copy in load(g):
            copy.wait()
        stores = store(g)
        stores[0].start()
        for l in range(g * group, (g + 1) * group):
            for c in range(node_blocks):
                some = pl.ds(c * LANES, LANES)
                average = (
                    own_v[l, :, some]
                    + coef[l] * packed_ref[c]
                    + coef[leaves + l] * packed_ref[node_blocks + c]
                )
                own_v[l, :, some] = average
                dual_v[l, :, some] = dual_v[l, :, some] + penalty * (x_v[l, :, some] - average)
        for copy in stores[1:]:
            copy.start()
    for g in range(groups):
        for copy in store(g):
            copy.wait()


def local(nf, ns, anchor, cost_lin, dual, target, leaf_weight, q_mat, diag_gain, block_mask, ancestor):
    leaves, sections, nodes = anchor.shape
    rows = leaves * sections
    blocks = nodes // LANES
    vmem, smem = pltpu.VMEM, pltpu.SMEM
    dma = pltpu.SemaphoreType.DMA
    cube = (leaves, sections, nodes)
    coef = (leaves, sections, LANES)
    piece = (blocks, sections, LANES)
    out = jax.ShapeDtypeStruct(cube, F32)
    hbm = pl.BlockSpec(memory_space=pltpu.HBM)
    far = pl.BlockSpec(memory_space=pl.ANY)
    near = pl.BlockSpec(memory_space=vmem)
    scalars = pl.BlockSpec(memory_space=smem)
    packed = jax.ShapeDtypeStruct((2 * blocks + 1, sections, LANES), F32)
    limit = 24 * 1024 * 1024
    state, own, parts = pl.pallas_call(
        functools.partial(kernel, nf, ns),
        out_shape=(out, out, packed),
        in_specs=[hbm, hbm, hbm, hbm, near, scalars, near, scalars, near],
        out_specs=(far, far, near),
        scratch_shapes=[
            vmem(cube, BF16), vmem(cube, BF16), vmem(cube, F32), vmem((nodes, nodes), BF16),
            vmem((nodes, nodes), BF16), vmem((rows, nodes), BF16), vmem((rows, nodes), F32), vmem((rows, nodes), F32),
            vmem((nodes, rows), F32), vmem((nodes, rows), F32), vmem((nodes, rows), F32),
            vmem((nodes, nodes), BF16), vmem((nodes, LANES), F32), vmem((rows, LANES), F32),
            vmem(cube, F32), vmem(cube, F32), vmem((LANES, LANES), F32),
            vmem(coef, F32), vmem(coef, F32),
            vmem((PROX_ITERS, 1, rows), F32), vmem((PROX_ITERS, nf - 1, 1, rows), F32),
            vmem((sections, LANES), F32), vmem((ns - 1, sections, LANES), F32),
            vmem(piece, F32), vmem(piece, F32), vmem(piece, F32), vmem(piece, F32),
            vmem(piece, F32), vmem(piece, F32),
            dma((4,)), dma((2,)), dma((PROX_ITERS,)), dma((PROX_ITERS,)), dma, dma,
            dma((blocks,)), dma((blocks,)), dma((blocks,)), dma((blocks,)),
        ],
        compiler_params=pltpu.CompilerParams(
            collective_id=0, has_side_effects=True, vmem_limit_bytes=limit
        ),
        cost_estimate=pl.CostEstimate(
            flops=2 * PROX_ITERS * rows * nodes * nodes, bytes_accessed=12 * rows * nodes, transcendentals=0
        ),
    )(*(pltpu.with_memory_space_constraint(v, pltpu.HBM) for v in (anchor, cost_lin, dual, q_mat)), target, leaf_weight, diag_gain.reshape(1, nodes), block_mask, ancestor.T)
    return pl.pallas_call(
        finish,
        out_shape=(out, out, out),
        in_specs=[far, far, far, near],
        out_specs=(far, far, far),
        scratch_shapes=[
            vmem(cube, F32), vmem(cube, F32), vmem(cube, F32),
            vmem((2 * leaves, sections, LANES), F32), dma((3 * leaves // 4,)), dma((3 * leaves // 4,)),
        ],
        compiler_params=pltpu.CompilerParams(vmem_limit_bytes=limit),
        cost_estimate=pl.CostEstimate(flops=8 * rows * nodes, bytes_accessed=24 * rows * nodes, transcendentals=0),
    )(state, own, dual, parts)


def solution(mesh):
    return jax.shard_map(
        functools.partial(local, mesh.shape["feeder"], mesh.shape["scen"]),
        mesh=mesh,
        in_specs=(
            P("scen", None, "feeder"),
            P("scen", None, "feeder"),
            P("scen", None, "feeder"),
            P("scen", None),
            P("scen"),
            P("feeder", None),
            P("feeder"),
            P("feeder", None, None),
            P(None, "scen"),
        ),
        out_specs=(P("scen", None, "feeder"), P("scen", None, "feeder"), P("scen", None, "feeder")),
        check_vma=False,
    )
```

```python
import functools

import jax
import jax.numpy as jnp
from jax import lax
from jax.experimental import pallas as pl
from jax.experimental.pallas import tpu as pltpu
from jax.sharding import PartitionSpec as P

PROX_ITERS = 8

penalty = 1.0
step_size = 0.08
coupling = 4.0
power_limit = 2.0

LANES = 128
MESH = pl.DeviceIdType.MESH
F32 = jnp.float32
BF16 = jnp.bfloat16


def kernel(
    nf, ns,
    anchor_hbm, cost_hbm, dual_hbm, q_hbm, target_hbm, weight_hbm, diag_hbm, mask_hbm, anc_hbm,
    x_out, own_out, packed_ref,
    target_ref, weight_ref, diag_ref, mask_ref, anc_ref,
    anchor_v, cost_v, dual_v, q_v, q_m, nat_b, nat, fixed_nat, xt, pre, fixed_t, q_t, gain_t, head_col,
    small, total_w, same,
    head_send, head_recv, note_send, note_recv, up_send, up_recv, down_send, down_recv, tail, front,
    in_sem, head_ssem, head_rsem, note_ssem, note_rsem, up_ssem, up_rsem, down_ssem, down_rsem,
):
    leaves, sections, nodes = x_out.shape
    rows = leaves * sections
    lane_blocks = rows // LANES
    node_blocks = nodes // LANES
    mf, ms = lax.axis_index("feeder"), lax.axis_index("scen")

    def partner(k):
        other, bit = mf, 1
        while bit < nf:
            if k & bit:
                other = other + bit - 2 * bit * lax.rem(lax.div(mf, bit), 2)
            bit *= 2
        return other

    order = sorted(range(1, nf), key=lambda k: -bin(k >> 1).count("1"))

    barrier = pltpu.get_barrier_semaphore()
    for k in range(1, nf):
        pl.semaphore_signal(barrier, inc=1, device_id=(partner(k), ms), device_id_type=MESH)
    for k in range(1, ns):
        pl.semaphore_signal(barrier, inc=1, device_id=(mf, lax.rem(ms + k, ns)), device_id_type=MESH)
    loads = [
        pltpu.make_async_copy(src, dst, in_sem.at[i])
        for i, (src, dst) in enumerate(
            (
                (anchor_hbm, anchor_v), (q_hbm, q_v), (cost_hbm, cost_v), (dual_hbm, dual_v),
                (target_hbm, target_ref), (weight_hbm, weight_ref), (diag_hbm, diag_ref),
                (mask_hbm, mask_ref), (anc_hbm, anc_ref),
            )
        )
    ]
    for load in loads:
        load.start()

    def leaf_rows(leaf):
        return pl.ds(leaf * sections, sections)

    def lanes(block):
        return pl.ds(block * LANES, LANES)

    def send_heads(step):
        for k in order:
            pltpu.make_async_remote_copy(
                src_ref=head_send.at[step],
                dst_ref=head_recv.at[step, k - 1],
                send_sem=head_ssem.at[step],
                recv_sem=head_rsem.at[step],
                device_id=(partner(k), ms),
                device_id_type=MESH,
            ).start()

    def head_term(step):
        got = head_recv.at[step]
        pltpu.make_async_copy(got, got, head_rsem.at[step]).wait()
        whole = head_send[step]
        for k in range(nf - 1):
            whole = whole + head_recv[step, k]
        return whole * (step_size * coupling / (nf * nodes))

    def window():
        image = jnp.dot(q_t[...], xt[...].astype(BF16), preferred_element_type=F32)
        for b in range(lane_blocks):
            cols = slice(b * LANES, (b + 1) * LANES)
            pre[:, cols] = gain_t[...] * xt[:, cols] - step_size * image[:, cols] - fixed_t[:, cols]

    loads[0].wait()
    for leaf in range(leaves):
        nat[leaf_rows(leaf), :] = anchor_v[leaf].astype(F32)
    nat_b[...] = nat[...].astype(BF16)
    ones = jnp.ones((8, nodes), BF16)
    sums = lax.dot_general(ones, nat_b[...], (((1,), (1,)), ((), ())), preferred_element_type=F32)
    head_send[0] = sums[0:1, :]
    pl.semaphore_wait(barrier, nf - 1 + ns - 1)
    send_heads(0)

    for load in loads[4:]:
        load.wait()
    small[...] = jnp.zeros_like(small)
    small[0:leaves, 0:sections] = anc_ref[...].astype(F32)
    small[leaves : 2 * leaves, 0:sections] = target_ref[...]
    small[...] = small[...].T
    loads[1].wait()
    for i in range(node_blocks):
        for j in range(node_blocks):
            q_m[lanes(i), lanes(j)] = q_v[lanes(i), lanes(j)] * mask_ref[0, i, j].astype(F32).astype(BF16)
    loads[2].wait()
    loads[3].wait()
    image = jnp.dot(nat_b[...], q_m[...], preferred_element_type=F32)
    gain_row = 1.0 - step_size * (2.0 * diag_ref[...] + penalty)
    for l in range(leaves):
        goal = small[0:sections, leaves + l : leaves + l + 1]
        here = nat[leaf_rows(l), :]
        fixed = step_size * (cost_v[l].astype(F32) + dual_v[l] - penalty * here - coupling * goal)
        fixed_nat[leaf_rows(l), :] = fixed
        nat[leaf_rows(l), :] = (
            gain_row * here - step_size * image[l * sections : (l + 1) * sections, :] - fixed
        )
    for b in range(lane_blocks):
        pre[:, lanes(b)] = nat[lanes(b), :].T

    def update(step):
        term = head_term(step - 1)
        part = jnp.zeros((8, rows), F32)
        for b in range(nodes // 64):
            some = slice(b * 64, (b + 1) * 64)
            new = jnp.clip(pre[some, :] - term, -power_limit, power_limit)
            xt[some, :] = new
            part = part + jnp.sum(new.reshape(8, 8, rows), axis=0)
        head_send[step] = jnp.sum(part, axis=0, keepdims=True)
        send_heads(step)

    def advance(step, carry):
        update(step)
        window()
        return carry

    update(1)
    q_t[...] = q_m[...].T
    for b in range(lane_blocks):
        fixed_t[:, lanes(b)] = fixed_nat[lanes(b), :].T
    gain_t[...] = jnp.broadcast_to(gain_row, (LANES, nodes)).T
    window()

    advance(2, 0)

    wide = (sections, LANES)

    def leaf_id(l):
        return jnp.broadcast_to(small[0:sections, l : l + 1], wide)

    ids = [leaf_id(l) for l in range(leaves)]
    run_w = [jnp.full(wide, weight_ref[0], F32)]
    for l in range(1, leaves):
        link = (ids[l] == ids[l - 1]).astype(F32)
        same[l] = link
        run_w.append(link * run_w[-1] + weight_ref[l])
    own_w = run_w[leaves - 1]
    total_w[leaves - 1] = own_w
    for l in range(leaves - 2, -1, -1):
        own_w = jnp.where(ids[l] == ids[l + 1], own_w, run_w[l])
        total_w[l] = own_w
    column = lax.broadcasted_iota(jnp.int32, wide, 1)
    note_send[...] = jnp.where(
        column == 0,
        run_w[leaves - 1],
        jnp.where(column == 1, ids[leaves - 1], jnp.where(column == 2, own_w, ids[0])),
    )
    for k in range(1, ns):
        pltpu.make_async_remote_copy(
            src_ref=note_send,
            dst_ref=note_recv.at[k - 1],
            send_sem=note_ssem,
            recv_sem=note_rsem,
            device_id=(mf, lax.rem(ms + k, ns)),
            device_id_type=MESH,
        ).start()

    lax.fori_loop(3, 5, advance, 0)

    pltpu.make_async_copy(note_recv, note_recv, note_rsem).wait()
    pltpu.make_async_copy(note_recv, note_recv, note_ssem).wait()
    first_id = leaf_id(0)
    last_id = leaf_id(leaves - 1)
    start = (ms * leaves).astype(F32)
    goes_back = (first_id < start).astype(F32)
    spans = (last_id < start).astype(F32)
    left_w = jnp.zeros(wide, F32)
    right_w = jnp.zeros(wide, F32)
    for k in range(1, ns):
        note = note_recv[k - 1]
        earlier = jnp.where(ms >= k, 1.0, 0.0)
        left_w += earlier * jnp.where(note[:, 1:2] == first_id, note[:, 0:1], 0.0)
        right_w += (1.0 - earlier) * jnp.where(note[:, 3:4] == last_id, note[:, 2:3], 0.0)
    packed = jnp.zeros(wide, F32)
    for l in range(leaves):
        own_id = leaf_id(l)
        in_first = (own_id == first_id).astype(F32)
        in_last = (own_id == last_id).astype(F32)
        scale = 1.0 / (total_w[l] + in_first * left_w + in_last * right_w)
        total_w[l] = scale
        packed = jnp.where(column == l, in_first * goes_back * scale, packed)
        packed = jnp.where(column == leaves + l, in_last * scale, packed)
    packed_ref[2 * node_blocks] = packed

    lax.fori_loop(5, PROX_ITERS, advance, 0)

    for b in range(lane_blocks):
        nat[lanes(b), :] = pre[:, lanes(b)].T
    term = head_term(PROX_ITERS - 1)
    for b in range(lane_blocks):
        head_col[lanes(b), :] = jnp.broadcast_to(term[:, b * LANES : (b + 1) * LANES], (LANES, LANES)).T

    def up_copy(c):
        return pltpu.make_async_remote_copy(
            src_ref=up_send.at[c], dst_ref=up_recv.at[c],
            send_sem=up_ssem.at[c], recv_sem=up_rsem.at[c],
            device_id=(mf, lax.rem(ms + 1, ns)), device_id_type=MESH,
        )

    def down_copy(c):
        return pltpu.make_async_remote_copy(
            src_ref=down_send.at[c], dst_ref=down_recv.at[c],
            send_sem=down_ssem.at[c], recv_sem=down_rsem.at[c],
            device_id=(mf, lax.rem(ms + ns - 1, ns)), device_id_type=MESH,
        )

    at_bottom, at_top = ms == 0, ms == ns - 1
    for c in range(node_blocks):
        run = None
        for l in range(leaves):
            x = jnp.clip(nat[leaf_rows(l), lanes(c)] - head_col[leaf_rows(l), :], -power_limit, power_limit)
            x_out[l, :, lanes(c)] = x
            weighted = weight_ref[l] * x
            if l == 0:
                run = weighted
                opening = weighted
                in_first = goes_back
            else:
                run = weighted + same[l] * run
                in_first = in_first * same[l]
                opening = opening + in_first * weighted
            own_out[l, :, lanes(c)] = run
        opening = opening * goes_back
        tail[c] = run
        front[c] = opening

        @pl.when(at_bottom)
        def _():
            up_send[c] = run
            up_copy(c).start()

        @pl.when(at_top)
        def _():
            down_send[c] = opening
            down_copy(c).start()

    for c in range(node_blocks):
        run = tail[c]
        for l in range(leaves - 1, -1, -1):
            if l < leaves - 1:
                run = jnp.where(same[l + 1] > 0.5, run, own_out[l, :, lanes(c)])
            own_out[l, :, lanes(c)] = run * total_w[l]

    def upward():
        for c in range(node_blocks):
            up_copy(c).wait_recv()

            @pl.when(jnp.logical_not(at_top))
            def _():
                up_send[c] = tail[c] + spans * up_recv[c]
                up_copy(c).start()

    def downward():
        for c in range(node_blocks):
            down_copy(c).wait_recv()

            @pl.when(jnp.logical_not(at_bottom))
            def _():
                down_send[c] = front[c] + spans * down_recv[c]
                down_copy(c).start()

    low = ms < ns // 2

    @pl.when(at_bottom)
    def _():
        up_recv[...] = jnp.zeros_like(up_recv)

    @pl.when(at_top)
    def _():
        down_recv[...] = jnp.zeros_like(down_recv)

    @pl.when(jnp.logical_and(low, jnp.logical_not(at_bottom)))
    def _():
        upward()

    @pl.when(jnp.logical_not(at_top))
    def _():
        downward()

    @pl.when(jnp.logical_not(low))
    def _():
        upward()

    for c in range(node_blocks):
        packed_ref[c] = up_recv[c]
        packed_ref[node_blocks + c] = down_recv[c]
    for c in range(node_blocks):

        @pl.when(jnp.logical_not(at_top))
        def _():
            up_copy(c).wait_send()

        @pl.when(jnp.logical_not(at_bottom))
        def _():
            down_copy(c).wait_send()

    for step in range(PROX_ITERS):
        pltpu.make_async_copy(head_recv.at[step], head_recv.at[step], head_ssem.at[step]).wait()


def finish(x_ref, own_ref, dual_ref, packed_ref, xout_hbm, avg_hbm, newdual_hbm, avg_v, new_v, coef, out_sem):
    leaves, sections, nodes = x_ref.shape
    node_blocks = nodes // LANES
    group = 4

    def store(first, i, src, dst):
        some = pl.ds(first, group)
        return pltpu.make_async_copy(src.at[some], dst.at[some], out_sem.at[3 * (first // group) + i])

    stores = [store(l, 0, x_ref, xout_hbm) for l in range(0, leaves, group)]
    for copy in stores:
        copy.start()
    packed = packed_ref[2 * node_blocks]
    for i in range(2 * leaves):
        coef[i] = jnp.broadcast_to(packed[:, i : i + 1], (sections, LANES))
    for l in range(leaves):
        for c in range(node_blocks):
            some = pl.ds(c * LANES, LANES)
            average = (
                own_ref[l, :, some]
                + coef[l] * packed_ref[c]
                + coef[leaves + l] * packed_ref[node_blocks + c]
            )
            avg_v[l, :, some] = average
            new_v[l, :, some] = dual_ref[l, :, some] + penalty * (x_ref[l, :, some] - average)
        if l % group == group - 1:
            first = l - group + 1
            for copy in (store(first, 1, avg_v, avg_hbm), store(first, 2, new_v, newdual_hbm)):
                copy.start()
                stores.append(copy)
    for copy in stores:
        copy.wait()


def local(nf, ns, anchor, cost_lin, dual, target, leaf_weight, q_mat, diag_gain, block_mask, ancestor):
    leaves, sections, nodes = anchor.shape
    rows = leaves * sections
    blocks = nodes // LANES
    vmem, smem = pltpu.VMEM, pltpu.SMEM
    dma = pltpu.SemaphoreType.DMA
    cube = (leaves, sections, nodes)
    coef = (leaves, sections, LANES)
    piece = (blocks, sections, LANES)
    out = jax.ShapeDtypeStruct(cube, F32)
    hbm = pl.BlockSpec(memory_space=pltpu.HBM)
    far = pl.BlockSpec(memory_space=pl.ANY)
    near = pl.BlockSpec(memory_space=vmem)
    packed = jax.ShapeDtypeStruct((2 * blocks + 1, sections, LANES), F32)
    limit = 24 * 1024 * 1024
    state, own, parts = pl.pallas_call(
        functools.partial(kernel, nf, ns),
        out_shape=(out, out, packed),
        in_specs=[hbm] * 9,
        out_specs=(near, near, near),
        scratch_shapes=[
            vmem((leaves, sections), F32), smem((leaves,), F32), vmem((1, nodes), F32),
            smem(block_mask.shape, jnp.int32), vmem((leaves, sections), jnp.int32),
            vmem(cube, BF16), vmem(cube, BF16), vmem(cube, F32), vmem((nodes, nodes), BF16),
            vmem((nodes, nodes), BF16), vmem((rows, nodes), BF16), vmem((rows, nodes), F32), vmem((rows, nodes), F32),
            vmem((nodes, rows), F32), vmem((nodes, rows), F32), vmem((nodes, rows), F32),
            vmem((nodes, nodes), BF16), vmem((nodes, LANES), F32), vmem((rows, LANES), F32),
            vmem((LANES, LANES), F32),
            vmem(coef, F32), vmem(coef, F32),
            vmem((PROX_ITERS, 1, rows), F32), vmem((PROX_ITERS, nf - 1, 1, rows), F32),
            vmem((sections, LANES), F32), vmem((ns - 1, sections, LANES), F32),
            vmem(piece, F32), vmem(piece, F32), vmem(piece, F32), vmem(piece, F32),
            vmem(piece, F32), vmem(piece, F32),
            dma((9,)), dma((PROX_ITERS,)), dma((PROX_ITERS,)), dma, dma,
            dma((blocks,)), dma((blocks,)), dma((blocks,)), dma((blocks,)),
        ],
        compiler_params=pltpu.CompilerParams(
            collective_id=0, has_side_effects=True, vmem_limit_bytes=limit
        ),
        cost_estimate=pl.CostEstimate(
            flops=2 * PROX_ITERS * rows * nodes * nodes, bytes_accessed=12 * rows * nodes, transcendentals=0
        ),
    )(
        *(
            pltpu.with_memory_space_constraint(array, pltpu.HBM)
            for array in (
                anchor, cost_lin, dual, q_mat, target, leaf_weight, diag_gain.reshape(1, nodes), block_mask,
                ancestor.T,
            )
        )
    )
    return pl.pallas_call(
        finish,
        out_shape=(out, out, out),
        in_specs=[near, near, near, near],
        out_specs=(far, far, far),
        scratch_shapes=[
            vmem(cube, F32), vmem(cube, F32), vmem((2 * leaves, sections, LANES), F32), dma((3 * leaves // 4,)),
        ],
        compiler_params=pltpu.CompilerParams(vmem_limit_bytes=limit),
        cost_estimate=pl.CostEstimate(flops=8 * rows * nodes, bytes_accessed=24 * rows * nodes, transcendentals=0),
    )(state, own, dual, parts)


def solution(mesh):
    return jax.shard_map(
        functools.partial(local, mesh.shape["feeder"], mesh.shape["scen"]),
        mesh=mesh,
        in_specs=(
            P("scen", None, "feeder"),
            P("scen", None, "feeder"),
            P("scen", None, "feeder"),
            P("scen", None),
            P("scen"),
            P("feeder", None),
            P("feeder"),
            P("feeder", None, None),
            P(None, "scen"),
        ),
        out_specs=(P("scen", None, "feeder"), P("scen", None, "feeder"), P("scen", None, "feeder")),
        check_vma=False,
    )
```

```python
import functools

import jax
import jax.numpy as jnp
from jax import lax
from jax.experimental import pallas as pl
from jax.experimental.pallas import tpu as pltpu
from jax.sharding import PartitionSpec as P

PROX_ITERS = 8

penalty = 1.0
step_size = 0.08
coupling = 4.0
power_limit = 2.0

LANES = 128
MESH = pl.DeviceIdType.MESH
F32 = jnp.float32
BF16 = jnp.bfloat16


def kernel(
    nf, ns,
    anchor_hbm, cost_hbm, dual_hbm, q_hbm, target_hbm, weight_hbm, diag_hbm, mask_hbm, anc_hbm,
    x_out, own_out, ends_out, coef_out,
    target_ref, weight_ref, diag_ref, mask_ref, anc_ref,
    anchor_v, cost_v, dual_v, q_v, q_m, nat_b, nat, fixed_nat, xt, xb, pre, fixed_t, q_t, gain_t, head_col,
    small, total_w, same,
    head_send, head_recv, note_send, note_recv, up_send, up_recv, down_send, down_recv, tail, front,
    in_sem, head_ssem, head_rsem, note_ssem, note_rsem, up_ssem, up_rsem, down_ssem, down_rsem,
):
    leaves, sections, nodes = x_out.shape
    rows = leaves * sections
    lane_blocks = rows // LANES
    node_blocks = nodes // LANES
    mf, ms = lax.axis_index("feeder"), lax.axis_index("scen")

    def partner(k):
        other, bit = mf, 1
        while bit < nf:
            if k & bit:
                other = other + bit - 2 * bit * lax.rem(lax.div(mf, bit), 2)
            bit *= 2
        return other

    order = sorted(range(1, nf), key=lambda k: -bin(k >> 1).count("1"))
    partners = {k: partner(k) for k in order}

    barrier = pltpu.get_barrier_semaphore()
    for k in range(1, nf):
        pl.semaphore_signal(barrier, inc=1, device_id=(partners[k], ms), device_id_type=MESH)
    for k in range(1, ns):
        pl.semaphore_signal(barrier, inc=1, device_id=(mf, lax.rem(ms + k, ns)), device_id_type=MESH)
    loads = [
        pltpu.make_async_copy(src, dst, in_sem.at[i])
        for i, (src, dst) in enumerate(
            (
                (anchor_hbm, anchor_v), (q_hbm, q_v), (cost_hbm, cost_v), (dual_hbm, dual_v),
                (target_hbm, target_ref), (weight_hbm, weight_ref), (diag_hbm, diag_ref),
                (mask_hbm, mask_ref), (anc_hbm, anc_ref),
            )
        )
    ]
    for load in loads:
        load.start()

    def leaf_rows(leaf):
        return pl.ds(leaf * sections, sections)

    def lanes(block):
        return pl.ds(block * LANES, LANES)

    def send_heads(step):
        for k in order:
            pltpu.make_async_remote_copy(
                src_ref=head_send.at[step],
                dst_ref=head_recv.at[step, k - 1],
                send_sem=head_ssem.at[step],
                recv_sem=head_rsem.at[step],
                device_id=(partners[k], ms),
                device_id_type=MESH,
            ).start()

    def head_term(step):
        got = head_recv.at[step]
        pltpu.make_async_copy(got, got, head_rsem.at[step]).wait()
        whole = head_send[step]
        for k in range(nf - 1):
            whole = whole + head_recv[step, k]
        return whole * (step_size * coupling / (nf * nodes))

    def window():
        for first in range(0, rows, 2 * LANES):
            last = min(first + 2 * LANES, rows)
            image = jnp.dot(q_t[...], xb[:, first:last], preferred_element_type=F32)
            for b in range(first, last, LANES):
                cols = slice(b, b + LANES)
                pre[:, cols] = (
                    gain_t[...] * xt[:, cols] - step_size * image[:, b - first : b - first + LANES] - fixed_t[:, cols]
                )

    loads[0].wait()
    for leaf in range(leaves):
        nat[leaf_rows(leaf), :] = anchor_v[leaf].astype(F32)
    nat_b[...] = nat[...].astype(BF16)
    ones = jnp.ones((8, nodes), BF16)
    sums = lax.dot_general(ones, nat_b[...], (((1,), (1,)), ((), ())), preferred_element_type=F32)
    head_send[0] = sums[0:1, :]
    pl.semaphore_wait(barrier, nf - 1 + ns - 1)
    send_heads(0)

    for load in loads[4:]:
        load.wait()
    small[...] = jnp.zeros_like(small)
    small[0:leaves, 0:sections] = anc_ref[...].astype(F32)
    small[leaves : 2 * leaves, 0:sections] = target_ref[...]
    small[...] = small[...].T
    loads[1].wait()
    for i in range(node_blocks):
        for j in range(node_blocks):
            q_m[lanes(i), lanes(j)] = q_v[lanes(i), lanes(j)] * mask_ref[0, i, j].astype(F32).astype(BF16)
    loads[2].wait()
    loads[3].wait()
    image = jnp.dot(nat_b[...], q_m[...], preferred_element_type=F32)
    gain_row = 1.0 - step_size * (2.0 * diag_ref[...] + penalty)
    for l in range(leaves):
        goal = small[0:sections, leaves + l : leaves + l + 1]
        here = nat[leaf_rows(l), :]
        fixed = step_size * (cost_v[l].astype(F32) + dual_v[l] - penalty * here - coupling * goal)
        fixed_nat[leaf_rows(l), :] = fixed
        nat[leaf_rows(l), :] = (
            gain_row * here - step_size * image[l * sections : (l + 1) * sections, :] - fixed
        )
    for b in range(lane_blocks):
        pre[:, lanes(b)] = nat[lanes(b), :].T

    def update(step):
        term = head_term(step - 1)
        part = jnp.zeros((8, rows), F32)
        for b in range(nodes // 64):
            some = slice(b * 64, (b + 1) * 64)
            new = jnp.clip(pre[some, :] - term, -power_limit, power_limit)
            xt[some, :] = new
            xb[some, :] = new.astype(BF16)
            part = part + jnp.sum(new.reshape(8, 8, rows), axis=0)
        head_send[step] = jnp.sum(part, axis=0, keepdims=True)
        send_heads(step)

    def advance(step, carry):
        update(step)
        window()
        return carry

    update(1)
    q_t[...] = q_m[...].T
    for b in range(lane_blocks):
        fixed_t[:, lanes(b)] = fixed_nat[lanes(b), :].T
    gain_t[...] = jnp.broadcast_to(gain_row, (LANES, nodes)).T
    window()

    advance(2, 0)

    wide = (sections, LANES)

    def leaf_id(l):
        return jnp.broadcast_to(small[0:sections, l : l + 1], wide)

    ids = [leaf_id(l) for l in range(leaves)]
    run_w = [jnp.full(wide, weight_ref[0], F32)]
    for l in range(1, leaves):
        link = (ids[l] == ids[l - 1]).astype(F32)
        same[l] = link
        run_w.append(link * run_w[-1] + weight_ref[l])
    own_w = run_w[leaves - 1]
    total_w[leaves - 1] = own_w
    for l in range(leaves - 2, -1, -1):
        own_w = jnp.where(ids[l] == ids[l + 1], own_w, run_w[l])
        total_w[l] = own_w
    column = lax.broadcasted_iota(jnp.int32, wide, 1)
    note_send[...] = jnp.where(
        column == 0,
        run_w[leaves - 1],
        jnp.where(column == 1, ids[leaves - 1], jnp.where(column == 2, own_w, ids[0])),
    )
    for k in range(1, ns):
        pltpu.make_async_remote_copy(
            src_ref=note_send,
            dst_ref=note_recv.at[k - 1],
            send_sem=note_ssem,
            recv_sem=note_rsem,
            device_id=(mf, lax.rem(ms + k, ns)),
            device_id_type=MESH,
        ).start()

    lax.fori_loop(3, 5, advance, 0)

    pltpu.make_async_copy(note_recv, note_recv, note_rsem).wait()
    pltpu.make_async_copy(note_recv, note_recv, note_ssem).wait()
    first_id = leaf_id(0)
    last_id = leaf_id(leaves - 1)
    start = (ms * leaves).astype(F32)
    goes_back = (first_id < start).astype(F32)
    spans = (last_id < start).astype(F32)
    left_w = jnp.zeros(wide, F32)
    right_w = jnp.zeros(wide, F32)
    for k in range(1, ns):
        note = note_recv[k - 1]
        earlier = jnp.where(ms >= k, 1.0, 0.0)
        left_w += earlier * jnp.where(note[:, 1:2] == first_id, note[:, 0:1], 0.0)
        right_w += (1.0 - earlier) * jnp.where(note[:, 3:4] == last_id, note[:, 2:3], 0.0)
    for l in range(leaves):
        own_id = leaf_id(l)
        in_first = (own_id == first_id).astype(F32)
        in_last = (own_id == last_id).astype(F32)
        scale = 1.0 / (total_w[l] + in_first * left_w + in_last * right_w)
        total_w[l] = scale
        coef_out[l] = in_first * goes_back * scale
        coef_out[leaves + l] = in_last * scale

    lax.fori_loop(5, PROX_ITERS, advance, 0)

    for b in range(lane_blocks):
        nat[lanes(b), :] = pre[:, lanes(b)].T
    term = head_term(PROX_ITERS - 1)
    for b in range(lane_blocks):
        head_col[lanes(b), :] = jnp.broadcast_to(term[:, b * LANES : (b + 1) * LANES], (LANES, LANES)).T

    def up_copy(c):
        return pltpu.make_async_remote_copy(
            src_ref=up_send.at[c], dst_ref=up_recv.at[c],
            send_sem=up_ssem.at[c], recv_sem=up_rsem.at[c],
            device_id=(mf, lax.rem(ms + 1, ns)), device_id_type=MESH,
        )

    def down_copy(c):
        return pltpu.make_async_remote_copy(
            src_ref=down_send.at[c], dst_ref=down_recv.at[c],
            send_sem=down_ssem.at[c], recv_sem=down_rsem.at[c],
            device_id=(mf, lax.rem(ms + ns - 1, ns)), device_id_type=MESH,
        )

    at_bottom, at_top = ms == 0, ms == ns - 1
    for c in range(node_blocks):
        run = None
        for l in range(leaves):
            x = jnp.clip(nat[leaf_rows(l), lanes(c)] - head_col[leaf_rows(l), :], -power_limit, power_limit)
            x_out[l, :, lanes(c)] = x
            weighted = weight_ref[l] * x
            if l == 0:
                run = weighted
                opening = weighted
                in_first = goes_back
            else:
                run = weighted + same[l] * run
                in_first = in_first * same[l]
                opening = opening + in_first * weighted
            own_out[l, :, lanes(c)] = run
        opening = opening * goes_back
        tail[c] = run
        front[c] = opening

        @pl.when(at_bottom)
        def _():
            up_send[c] = run
            up_copy(c).start()

        @pl.when(at_top)
        def _():
            down_send[c] = opening
            down_copy(c).start()

    for c in range(node_blocks):
        run = tail[c]
        for l in range(leaves - 1, -1, -1):
            if l < leaves - 1:
                run = jnp.where(same[l + 1] > 0.5, run, own_out[l, :, lanes(c)])
            own_out[l, :, lanes(c)] = run * total_w[l]

    def upward():
        for c in range(node_blocks):
            up_copy(c).wait_recv()

            @pl.when(jnp.logical_not(at_top))
            def _():
                up_send[c] = tail[c] + spans * up_recv[c]
                up_copy(c).start()

    def downward():
        for c in range(node_blocks):
            down_copy(c).wait_recv()

            @pl.when(jnp.logical_not(at_bottom))
            def _():
                down_send[c] = front[c] + spans * down_recv[c]
                down_copy(c).start()

    low = ms < ns // 2

    @pl.when(at_bottom)
    def _():
        up_recv[...] = jnp.zeros_like(up_recv)

    @pl.when(at_top)
    def _():
        down_recv[...] = jnp.zeros_like(down_recv)

    @pl.when(jnp.logical_and(low, jnp.logical_not(at_bottom)))
    def _():
        upward()

    @pl.when(jnp.logical_not(at_top))
    def _():
        downward()

    @pl.when(jnp.logical_not(low))
    def _():
        upward()

    for c in range(node_blocks):
        ends_out[c] = up_recv[c]
        ends_out[node_blocks + c] = down_recv[c]
    for c in range(node_blocks):

        @pl.when(jnp.logical_not(at_top))
        def _():
            up_copy(c).wait_send()

        @pl.when(jnp.logical_not(at_bottom))
        def _():
            down_copy(c).wait_send()

    for step in range(PROX_ITERS):
        pltpu.make_async_copy(head_recv.at[step], head_recv.at[step], head_ssem.at[step]).wait()


def finish(x_ref, own_ref, dual_ref, ends, coef, xout_hbm, avg_hbm, newdual_hbm, avg_v, new_v, out_sem):
    leaves, sections, nodes = x_ref.shape
    node_blocks = nodes // LANES
    group = 4

    def store(first, i, src, dst):
        some = pl.ds(first, group)
        return pltpu.make_async_copy(src.at[some], dst.at[some], out_sem.at[3 * (first // group) + i])

    stores = [store(l, 0, x_ref, xout_hbm) for l in range(0, leaves, group)]
    for copy in stores:
        copy.start()
    for l in range(leaves):
        for c in range(node_blocks):
            some = pl.ds(c * LANES, LANES)
            average = (
                own_ref[l, :, some] + coef[l] * ends[c] + coef[leaves + l] * ends[node_blocks + c]
            )
            avg_v[l, :, some] = average
            new_v[l, :, some] = dual_ref[l, :, some] + penalty * (x_ref[l, :, some] - average)
        if l % group == group - 1:
            first = l - group + 1
            for copy in (store(first, 1, avg_v, avg_hbm), store(first, 2, new_v, newdual_hbm)):
                copy.start()
                stores.append(copy)
    for copy in stores:
        copy.wait()


def local(nf, ns, anchor, cost_lin, dual, target, leaf_weight, q_mat, diag_gain, block_mask, ancestor):
    leaves, sections, nodes = anchor.shape
    rows = leaves * sections
    blocks = nodes // LANES
    vmem, smem = pltpu.VMEM, pltpu.SMEM
    dma = pltpu.SemaphoreType.DMA
    cube = (leaves, sections, nodes)
    coef = (leaves, sections, LANES)
    piece = (blocks, sections, LANES)
    out = jax.ShapeDtypeStruct(cube, F32)
    hbm = pl.BlockSpec(memory_space=pltpu.HBM)
    far = pl.BlockSpec(memory_space=pl.ANY)
    near = pl.BlockSpec(memory_space=vmem)
    sums = jax.ShapeDtypeStruct((2 * blocks, sections, LANES), F32)
    shares = jax.ShapeDtypeStruct((2 * leaves, sections, LANES), F32)
    limit = 24 * 1024 * 1024
    state, own, parts, factors = pl.pallas_call(
        functools.partial(kernel, nf, ns),
        out_shape=(out, out, sums, shares),
        in_specs=[hbm] * 9,
        out_specs=(near, near, near, near),
        scratch_shapes=[
            vmem((leaves, sections), F32), smem((leaves,), F32), vmem((1, nodes), F32),
            smem(block_mask.shape, jnp.int32), vmem((leaves, sections), jnp.int32),
            vmem(cube, BF16), vmem(cube, BF16), vmem(cube, F32), vmem((nodes, nodes), BF16),
            vmem((nodes, nodes), BF16), vmem((rows, nodes), BF16), vmem((rows, nodes), F32), vmem((rows, nodes), F32),
            vmem((nodes, rows), F32), vmem((nodes, rows), BF16), vmem((nodes, rows), F32), vmem((nodes, rows), F32),
            vmem((nodes, nodes), BF16), vmem((nodes, LANES), F32), vmem((rows, LANES), F32),
            vmem((LANES, LANES), F32),
            vmem(coef, F32), vmem(coef, F32),
            vmem((PROX_ITERS, 1, rows), F32), vmem((PROX_ITERS, nf - 1, 1, rows), F32),
            vmem((sections, LANES), F32), vmem((ns - 1, sections, LANES), F32),
            vmem(piece, F32), vmem(piece, F32), vmem(piece, F32), vmem(piece, F32),
            vmem(piece, F32), vmem(piece, F32),
            dma((9,)), dma((PROX_ITERS,)), dma((PROX_ITERS,)), dma, dma,
            dma((blocks,)), dma((blocks,)), dma((blocks,)), dma((blocks,)),
        ],
        compiler_params=pltpu.CompilerParams(
            collective_id=0, has_side_effects=True, vmem_limit_bytes=limit
        ),
        cost_estimate=pl.CostEstimate(
            flops=2 * PROX_ITERS * rows * nodes * nodes, bytes_accessed=12 * rows * nodes, transcendentals=0
        ),
    )(
        *(
            pltpu.with_memory_space_constraint(array, pltpu.HBM)
            for array in (
                anchor, cost_lin, dual, q_mat, target, leaf_weight, diag_gain.reshape(1, nodes), block_mask,
                ancestor.T,
            )
        )
    )
    return pl.pallas_call(
        finish,
        out_shape=(out, out, out),
        in_specs=[near, near, near, near, near],
        out_specs=(far, far, far),
        scratch_shapes=[
            vmem(cube, F32), vmem(cube, F32), dma((3 * leaves // 4,)),
        ],
        compiler_params=pltpu.CompilerParams(vmem_limit_bytes=limit),
        cost_estimate=pl.CostEstimate(flops=8 * rows * nodes, bytes_accessed=24 * rows * nodes, transcendentals=0),
    )(state, own, dual, parts, factors)


def solution(mesh):
    return jax.shard_map(
        functools.partial(local, mesh.shape["feeder"], mesh.shape["scen"]),
        mesh=mesh,
        in_specs=(
            P("scen", None, "feeder"),
            P("scen", None, "feeder"),
            P("scen", None, "feeder"),
            P("scen", None),
            P("scen"),
            P("feeder", None),
            P("feeder"),
            P("feeder", None, None),
            P(None, "scen"),
        ),
        out_specs=(P("scen", None, "feeder"), P("scen", None, "feeder"), P("scen", None, "feeder")),
        check_vma=False,
    )
```

```python
import functools

import jax
import jax.numpy as jnp
from jax import lax
from jax.experimental import pallas as pl
from jax.experimental.pallas import tpu as pltpu
from jax.sharding import PartitionSpec as P

PROX_ITERS = 8

penalty = 1.0
step_size = 0.08
coupling = 4.0
power_limit = 2.0

LANES = 128
MESH = pl.DeviceIdType.MESH
F32 = jnp.float32
BF16 = jnp.bfloat16


def kernel(
    nf, ns,
    anchor_hbm, cost_hbm, dual_hbm, q_hbm, target_hbm, weight_hbm, diag_hbm, mask_hbm, anc_hbm,
    x_out, own_out, packed_ref,
    target_ref, weight_ref, diag_ref, mask_ref, anc_ref,
    anchor_v, cost_v, dual_v, q_v, q_m, nat_b, nat, fixed_nat, xt, pre, fixed_t, q_t, gain_t, head_col,
    small, total_w, same,
    head_send, head_recv, head_all, note_send, note_recv, up_send, up_recv, down_send, down_recv, tail, front,
    in_sem, head_ssem, head_rsem, all_rsem, note_ssem, note_rsem, up_ssem, up_rsem, down_ssem, down_rsem,
):
    leaves, sections, nodes = x_out.shape
    rows = leaves * sections
    lane_blocks = rows // LANES
    node_blocks = nodes // LANES
    mf, ms = lax.axis_index("feeder"), lax.axis_index("scen")

    def partner(k):
        other, bit = mf, 1
        while bit < nf:
            if k & bit:
                other = other + bit - 2 * bit * lax.rem(lax.div(mf, bit), 2)
            bit *= 2
        return other

    order = sorted(range(1, nf), key=lambda k: -bin(k >> 1).count("1"))
    partners = {k: partner(k) for k in order}

    barrier = pltpu.get_barrier_semaphore()
    for k in range(1, nf):
        pl.semaphore_signal(barrier, inc=1, device_id=(partners[k], ms), device_id_type=MESH)
    for k in range(1, ns):
        pl.semaphore_signal(barrier, inc=1, device_id=(mf, lax.rem(ms + k, ns)), device_id_type=MESH)
    loads = [
        pltpu.make_async_copy(src, dst, in_sem.at[i])
        for i, (src, dst) in enumerate(
            (
                (anchor_hbm, anchor_v), (q_hbm, q_v), (cost_hbm, cost_v), (dual_hbm, dual_v),
                (target_hbm, target_ref), (weight_hbm, weight_ref), (diag_hbm, diag_ref),
                (mask_hbm, mask_ref), (anc_hbm, anc_ref),
            )
        )
    ]
    for load in loads:
        load.start()

    def leaf_rows(leaf):
        return pl.ds(leaf * sections, sections)

    def lanes(block):
        return pl.ds(block * LANES, LANES)

    second = lax.rem(mf, 2) == 1
    first = jnp.logical_not(second)

    def send_heads(step):
        def to(k):
            pltpu.make_async_remote_copy(
                src_ref=head_send.at[step],
                dst_ref=head_recv.at[step, k - 1],
                send_sem=head_ssem.at[step],
                recv_sem=head_rsem.at[step],
                device_id=(partners[k], ms),
                device_id_type=MESH,
            ).start()

        @pl.when(first)
        def _():
            for k in order:
                if k % 2 == 1:
                    to(k)

        @pl.when(second)
        def _():
            for k in order:
                if k % 2 == 0:
                    to(k)

    def head_term(step):
        @pl.when(second)
        def _():
            got = head_recv.at[step]
            pltpu.make_async_copy(got, got, head_rsem.at[step]).wait()
            whole = head_send[step]
            for k in range(nf - 1):
                whole = whole + head_recv[step, k]
            head_all[step] = whole
            pltpu.make_async_remote_copy(
                src_ref=head_all.at[step],
                dst_ref=head_all.at[step],
                send_sem=head_ssem.at[step],
                recv_sem=all_rsem.at[step],
                device_id=(partners[1], ms),
                device_id_type=MESH,
            ).start()

        @pl.when(first)
        def _():
            pltpu.make_async_copy(head_all.at[step], head_all.at[step], all_rsem.at[step]).wait()

        return head_all[step] * (step_size * coupling / (nf * nodes))

    def window():
        image = jnp.dot(q_t[...], xt[...].astype(BF16), preferred_element_type=F32)
        for b in range(lane_blocks):
            cols = slice(b * LANES, (b + 1) * LANES)
            pre[:, cols] = gain_t[...] * xt[:, cols] - step_size * image[:, cols] - fixed_t[:, cols]

    loads[0].wait()
    for leaf in range(leaves):
        nat[leaf_rows(leaf), :] = anchor_v[leaf].astype(F32)
    nat_b[...] = nat[...].astype(BF16)
    ones = jnp.ones((8, nodes), BF16)
    sums = lax.dot_general(ones, nat_b[...], (((1,), (1,)), ((), ())), preferred_element_type=F32)
    head_send[0] = sums[0:1, :]
    pl.semaphore_wait(barrier, nf - 1 + ns - 1)
    send_heads(0)

    for load in loads[4:]:
        load.wait()
    small[...] = jnp.zeros_like(small)
    small[0:leaves, 0:sections] = anc_ref[...].astype(F32)
    small[leaves : 2 * leaves, 0:sections] = target_ref[...]
    small[...] = small[...].T
    loads[1].wait()
    for i in range(node_blocks):
        for j in range(node_blocks):
            q_m[lanes(i), lanes(j)] = q_v[lanes(i), lanes(j)] * mask_ref[0, i, j].astype(F32).astype(BF16)
    loads[2].wait()
    loads[3].wait()
    image = jnp.dot(nat_b[...], q_m[...], preferred_element_type=F32)
    gain_row = 1.0 - step_size * (2.0 * diag_ref[...] + penalty)
    for l in range(leaves):
        goal = small[0:sections, leaves + l : leaves + l + 1]
        here = nat[leaf_rows(l), :]
        fixed = step_size * (cost_v[l].astype(F32) + dual_v[l] - penalty * here - coupling * goal)
        fixed_nat[leaf_rows(l), :] = fixed
        nat[leaf_rows(l), :] = (
            gain_row * here - step_size * image[l * sections : (l + 1) * sections, :] - fixed
        )
    for b in range(lane_blocks):
        pre[:, lanes(b)] = nat[lanes(b), :].T

    def update(step):
        term = head_term(step - 1)
        part = jnp.zeros((8, rows), F32)
        for b in range(nodes // 64):
            some = slice(b * 64, (b + 1) * 64)
            new = jnp.clip(pre[some, :] - term, -power_limit, power_limit)
            xt[some, :] = new
            part = part + jnp.sum(new.reshape(8, 8, rows), axis=0)
        head_send[step] = jnp.sum(part, axis=0, keepdims=True)
        send_heads(step)

    def advance(step, carry):
        update(step)
        window()
        return carry

    update(1)
    q_t[...] = q_m[...].T
    for b in range(lane_blocks):
        fixed_t[:, lanes(b)] = fixed_nat[lanes(b), :].T
    gain_t[...] = jnp.broadcast_to(gain_row, (LANES, nodes)).T
    window()

    advance(2, 0)

    wide = (sections, LANES)

    def leaf_id(l):
        return jnp.broadcast_to(small[0:sections, l : l + 1], wide)

    ids = [leaf_id(l) for l in range(leaves)]
    run_w = [jnp.full(wide, weight_ref[0], F32)]
    for l in range(1, leaves):
        link = (ids[l] == ids[l - 1]).astype(F32)
        same[l] = link
        run_w.append(link * run_w[-1] + weight_ref[l])
    own_w = run_w[leaves - 1]
    total_w[leaves - 1] = own_w
    for l in range(leaves - 2, -1, -1):
        own_w = jnp.where(ids[l] == ids[l + 1], own_w, run_w[l])
        total_w[l] = own_w
    column = lax.broadcasted_iota(jnp.int32, wide, 1)
    note_send[...] = jnp.where(
        column == 0,
        run_w[leaves - 1],
        jnp.where(column == 1, ids[leaves - 1], jnp.where(column == 2, own_w, ids[0])),
    )
    for k in range(1, ns):
        pltpu.make_async_remote_copy(
            src_ref=note_send,
            dst_ref=note_recv.at[k - 1],
            send_sem=note_ssem,
            recv_sem=note_rsem,
            device_id=(mf, lax.rem(ms + k, ns)),
            device_id_type=MESH,
        ).start()

    lax.fori_loop(3, 5, advance, 0)

    pltpu.make_async_copy(note_recv, note_recv, note_rsem).wait()
    pltpu.make_async_copy(note_recv, note_recv, note_ssem).wait()
    first_id = leaf_id(0)
    last_id = leaf_id(leaves - 1)
    start = (ms * leaves).astype(F32)
    goes_back = (first_id < start).astype(F32)
    spans = (last_id < start).astype(F32)
    left_w = jnp.zeros(wide, F32)
    right_w = jnp.zeros(wide, F32)
    for k in range(1, ns):
        note = note_recv[k - 1]
        earlier = jnp.where(ms >= k, 1.0, 0.0)
        left_w += earlier * jnp.where(note[:, 1:2] == first_id, note[:, 0:1], 0.0)
        right_w += (1.0 - earlier) * jnp.where(note[:, 3:4] == last_id, note[:, 2:3], 0.0)
    packed = jnp.zeros(wide, F32)
    for l in range(leaves):
        own_id = leaf_id(l)
        in_first = (own_id == first_id).astype(F32)
        in_last = (own_id == last_id).astype(F32)
        scale = 1.0 / (total_w[l] + in_first * left_w + in_last * right_w)
        total_w[l] = scale
        packed = jnp.where(column == l, in_first * goes_back * scale, packed)
        packed = jnp.where(column == leaves + l, in_last * scale, packed)
    packed_ref[2 * node_blocks] = packed

    lax.fori_loop(5, PROX_ITERS, advance, 0)

    for b in range(lane_blocks):
        nat[lanes(b), :] = pre[:, lanes(b)].T
    term = head_term(PROX_ITERS - 1)
    for b in range(lane_blocks):
        head_col[lanes(b), :] = jnp.broadcast_to(term[:, b * LANES : (b + 1) * LANES], (LANES, LANES)).T

    def up_copy(c):
        return pltpu.make_async_remote_copy(
            src_ref=up_send.at[c], dst_ref=up_recv.at[c],
            send_sem=up_ssem.at[c], recv_sem=up_rsem.at[c],
            device_id=(mf, lax.rem(ms + 1, ns)), device_id_type=MESH,
        )

    def down_copy(c):
        return pltpu.make_async_remote_copy(
            src_ref=down_send.at[c], dst_ref=down_recv.at[c],
            send_sem=down_ssem.at[c], recv_sem=down_rsem.at[c],
            device_id=(mf, lax.rem(ms + ns - 1, ns)), device_id_type=MESH,
        )

    at_bottom, at_top = ms == 0, ms == ns - 1
    for c in range(node_blocks):
        run = None
        for l in range(leaves):
            x = jnp.clip(nat[leaf_rows(l), lanes(c)] - head_col[leaf_rows(l), :], -power_limit, power_limit)
            x_out[l, :, lanes(c)] = x
            weighted = weight_ref[l] * x
            if l == 0:
                run = weighted
                opening = weighted
                in_first = goes_back
            else:
                run = weighted + same[l] * run
                in_first = in_first * same[l]
                opening = opening + in_first * weighted
            own_out[l, :, lanes(c)] = run
        opening = opening * goes_back
        tail[c] = run
        front[c] = opening

        @pl.when(at_bottom)
        def _():
            up_send[c] = run
            up_copy(c).start()

        @pl.when(at_top)
        def _():
            down_send[c] = opening
            down_copy(c).start()

    for c in range(node_blocks):
        run = tail[c]
        for l in range(leaves - 1, -1, -1):
            if l < leaves - 1:
                run = jnp.where(same[l + 1] > 0.5, run, own_out[l, :, lanes(c)])
            own_out[l, :, lanes(c)] = run * total_w[l]

    def upward():
        for c in range(node_blocks):
            up_copy(c).wait_recv()

            @pl.when(jnp.logical_not(at_top))
            def _():
                up_send[c] = tail[c] + spans * up_recv[c]
                up_copy(c).start()

    def downward():
        for c in range(node_blocks):
            down_copy(c).wait_recv()

            @pl.when(jnp.logical_not(at_bottom))
            def _():
                down_send[c] = front[c] + spans * down_recv[c]
                down_copy(c).start()

    low = ms < ns // 2

    @pl.when(at_bottom)
    def _():
        up_recv[...] = jnp.zeros_like(up_recv)

    @pl.when(at_top)
    def _():
        down_recv[...] = jnp.zeros_like(down_recv)

    @pl.when(jnp.logical_and(low, jnp.logical_not(at_bottom)))
    def _():
        upward()

    @pl.when(jnp.logical_not(at_top))
    def _():
        downward()

    @pl.when(jnp.logical_not(low))
    def _():
        upward()

    for c in range(node_blocks):
        packed_ref[c] = up_recv[c]
        packed_ref[node_blocks + c] = down_recv[c]
    for c in range(node_blocks):

        @pl.when(jnp.logical_not(at_top))
        def _():
            up_copy(c).wait_send()

        @pl.when(jnp.logical_not(at_bottom))
        def _():
            down_copy(c).wait_send()

    for step in range(PROX_ITERS):
        sent = head_recv.at[step, pl.ds(0, nf // 2)]
        pltpu.make_async_copy(sent, sent, head_ssem.at[step]).wait()


def finish(x_ref, own_ref, dual_ref, packed_ref, xout_hbm, avg_hbm, newdual_hbm, avg_v, new_v, coef, out_sem):
    leaves, sections, nodes = x_ref.shape
    node_blocks = nodes // LANES
    group = 4

    def store(first, i, src, dst):
        some = pl.ds(first, group)
        return pltpu.make_async_copy(src.at[some], dst.at[some], out_sem.at[3 * (first // group) + i])

    stores = [store(l, 0, x_ref, xout_hbm) for l in range(0, leaves, group)]
    for copy in stores:
        copy.start()
    packed = packed_ref[2 * node_blocks]
    for i in range(2 * leaves):
        coef[i] = jnp.broadcast_to(packed[:, i : i + 1], (sections, LANES))
    for l in range(leaves):
        for c in range(node_blocks):
            some = pl.ds(c * LANES, LANES)
            average = (
                own_ref[l, :, some]
                + coef[l] * packed_ref[c]
                + coef[leaves + l] * packed_ref[node_blocks + c]
            )
            avg_v[l, :, some] = average
            new_v[l, :, some] = dual_ref[l, :, some] + penalty * (x_ref[l, :, some] - average)
        if l % group == group - 1:
            first = l - group + 1
            for copy in (store(first, 1, avg_v, avg_hbm), store(first, 2, new_v, newdual_hbm)):
                copy.start()
                stores.append(copy)
    for copy in stores:
        copy.wait()


def local(nf, ns, anchor, cost_lin, dual, target, leaf_weight, q_mat, diag_gain, block_mask, ancestor):
    leaves, sections, nodes = anchor.shape
    rows = leaves * sections
    blocks = nodes // LANES
    vmem, smem = pltpu.VMEM, pltpu.SMEM
    dma = pltpu.SemaphoreType.DMA
    cube = (leaves, sections, nodes)
    coef = (leaves, sections, LANES)
    piece = (blocks, sections, LANES)
    out = jax.ShapeDtypeStruct(cube, F32)
    hbm = pl.BlockSpec(memory_space=pltpu.HBM)
    far = pl.BlockSpec(memory_space=pl.ANY)
    near = pl.BlockSpec(memory_space=vmem)
    packed = jax.ShapeDtypeStruct((2 * blocks + 1, sections, LANES), F32)
    limit = 24 * 1024 * 1024
    state, own, parts = pl.pallas_call(
        functools.partial(kernel, nf, ns),
        out_shape=(out, out, packed),
        in_specs=[hbm] * 9,
        out_specs=(near, near, near),
        scratch_shapes=[
            vmem((leaves, sections), F32), smem((leaves,), F32), vmem((1, nodes), F32),
            smem(block_mask.shape, jnp.int32), vmem((leaves, sections), jnp.int32),
            vmem(cube, BF16), vmem(cube, BF16), vmem(cube, F32), vmem((nodes, nodes), BF16),
            vmem((nodes, nodes), BF16), vmem((rows, nodes), BF16), vmem((rows, nodes), F32), vmem((rows, nodes), F32),
            vmem((nodes, rows), F32), vmem((nodes, rows), F32), vmem((nodes, rows), F32),
            vmem((nodes, nodes), BF16), vmem((nodes, LANES), F32), vmem((rows, LANES), F32),
            vmem((LANES, LANES), F32),
            vmem(coef, F32), vmem(coef, F32),
            vmem((PROX_ITERS, 1, rows), F32), vmem((PROX_ITERS, nf - 1, 1, rows), F32),
            vmem((PROX_ITERS, 1, rows), F32),
            vmem((sections, LANES), F32), vmem((ns - 1, sections, LANES), F32),
            vmem(piece, F32), vmem(piece, F32), vmem(piece, F32), vmem(piece, F32),
            vmem(piece, F32), vmem(piece, F32),
            dma((9,)), dma((PROX_ITERS,)), dma((PROX_ITERS,)), dma((PROX_ITERS,)), dma, dma,
            dma((blocks,)), dma((blocks,)), dma((blocks,)), dma((blocks,)),
        ],
        compiler_params=pltpu.CompilerParams(
            collective_id=0, has_side_effects=True, vmem_limit_bytes=limit
        ),
        cost_estimate=pl.CostEstimate(
            flops=2 * PROX_ITERS * rows * nodes * nodes, bytes_accessed=12 * rows * nodes, transcendentals=0
        ),
    )(
        *(
            pltpu.with_memory_space_constraint(array, pltpu.HBM)
            for array in (
                anchor, cost_lin, dual, q_mat, target, leaf_weight, diag_gain.reshape(1, nodes), block_mask,
                ancestor.T,
            )
        )
    )
    return pl.pallas_call(
        finish,
        out_shape=(out, out, out),
        in_specs=[near, near, near, near],
        out_specs=(far, far, far),
        scratch_shapes=[
            vmem(cube, F32), vmem(cube, F32), vmem((2 * leaves, sections, LANES), F32), dma((3 * leaves // 4,)),
        ],
        compiler_params=pltpu.CompilerParams(vmem_limit_bytes=limit),
        cost_estimate=pl.CostEstimate(flops=8 * rows * nodes, bytes_accessed=24 * rows * nodes, transcendentals=0),
    )(state, own, dual, parts)


def solution(mesh):
    return jax.shard_map(
        functools.partial(local, mesh.shape["feeder"], mesh.shape["scen"]),
        mesh=mesh,
        in_specs=(
            P("scen", None, "feeder"),
            P("scen", None, "feeder"),
            P("scen", None, "feeder"),
            P("scen", None),
            P("scen"),
            P("feeder", None),
            P("feeder"),
            P("feeder", None, None),
            P(None, "scen"),
        ),
        out_specs=(P("scen", None, "feeder"), P("scen", None, "feeder"), P("scen", None, "feeder")),
        check_vma=False,
    )
```

```python
import functools

import jax
import jax.numpy as jnp
from jax import lax
from jax.experimental import pallas as pl
from jax.experimental.pallas import tpu as pltpu
from jax.sharding import PartitionSpec as P

PROX_ITERS = 8

penalty = 1.0
step_size = 0.08
coupling = 4.0
power_limit = 2.0

LANES = 128
MESH = pl.DeviceIdType.MESH
F32 = jnp.float32
BF16 = jnp.bfloat16


def kernel(
    nf, ns,
    anchor_hbm, cost_hbm, dual_hbm, q_hbm, target_hbm, weight_hbm, diag_hbm, mask_hbm, anc_hbm,
    x_out, own_out, packed_ref,
    target_ref, weight_ref, diag_ref, mask_ref, anc_ref,
    anchor_v, cost_v, dual_v, q_v, q_m, nat_b, nat, fixed_nat, xt, pre, fixed_t, q_t, gain_t, head_col,
    small, total_w, same,
    head_send, head_recv, note_send, note_recv, up_send, up_recv, down_send, down_recv, tail, front,
    in_sem, head_ssem, head_rsem, note_ssem, note_rsem, up_ssem, up_rsem, down_ssem, down_rsem,
):
    leaves, sections, nodes = x_out.shape
    rows = leaves * sections
    lane_blocks = rows // LANES
    node_blocks = nodes // LANES
    mf, ms = lax.axis_index("feeder"), lax.axis_index("scen")

    def partner(k):
        other, bit = mf, 1
        while bit < nf:
            if k & bit:
                other = other + bit - 2 * bit * lax.rem(lax.div(mf, bit), 2)
            bit *= 2
        return other

    order = sorted(range(1, nf), key=lambda k: -bin(k >> 1).count("1"))

    barrier = pltpu.get_barrier_semaphore()
    for k in range(1, nf):
        pl.semaphore_signal(barrier, inc=1, device_id=(partner(k), ms), device_id_type=MESH)
    for k in range(1, ns):
        pl.semaphore_signal(barrier, inc=1, device_id=(mf, lax.rem(ms + k, ns)), device_id_type=MESH)
    loads = [
        pltpu.make_async_copy(src, dst, in_sem.at[i])
        for i, (src, dst) in enumerate(
            (
                (anchor_hbm, anchor_v), (q_hbm, q_v), (cost_hbm, cost_v), (dual_hbm, dual_v),
                (target_hbm, target_ref), (weight_hbm, weight_ref), (diag_hbm, diag_ref),
                (mask_hbm, mask_ref), (anc_hbm, anc_ref),
            )
        )
    ]
    for load in loads:
        load.start()

    def leaf_rows(leaf):
        return pl.ds(leaf * sections, sections)

    def lanes(block):
        return pl.ds(block * LANES, LANES)

    def send_heads(step):
        for k in order:
            pltpu.make_async_remote_copy(
                src_ref=head_send.at[step],
                dst_ref=head_recv.at[step, k - 1],
                send_sem=head_ssem.at[step],
                recv_sem=head_rsem.at[step],
                device_id=(partner(k), ms),
                device_id_type=MESH,
            ).start()

    def head_term(step):
        got = head_recv.at[step]
        pltpu.make_async_copy(got, got, head_rsem.at[step]).wait()
        whole = head_send[step]
        for k in range(nf - 1):
            whole = whole + head_recv[step, k]
        return whole * (step_size * coupling / (nf * nodes))

    def window():
        image = jnp.dot(q_t[...], xt[...].astype(BF16), preferred_element_type=F32)
        for b in range(lane_blocks):
            cols = slice(b * LANES, (b + 1) * LANES)
            pre[:, cols] = gain_t[...] * xt[:, cols] - step_size * image[:, cols] - fixed_t[:, cols]

    loads[0].wait()
    for leaf in range(leaves):
        nat[leaf_rows(leaf), :] = anchor_v[leaf].astype(F32)
    nat_b[...] = nat[...].astype(BF16)
    ones = jnp.ones((8, nodes), BF16)
    sums = lax.dot_general(ones, nat_b[...], (((1,), (1,)), ((), ())), preferred_element_type=F32)
    head_send[0] = sums[0:1, :]
    pl.semaphore_wait(barrier, nf - 1 + ns - 1)
    send_heads(0)

    for load in loads[4:]:
        load.wait()
    small[...] = jnp.zeros_like(small)
    small[0:leaves, 0:sections] = anc_ref[...].astype(F32)
    small[leaves : 2 * leaves, 0:sections] = target_ref[...]
    small[...] = small[...].T
    loads[1].wait()
    for i in range(node_blocks):
        for j in range(node_blocks):
            q_m[lanes(i), lanes(j)] = q_v[lanes(i), lanes(j)] * mask_ref[0, i, j].astype(F32).astype(BF16)
    loads[2].wait()
    loads[3].wait()
    image = jnp.dot(nat_b[...], q_m[...], preferred_element_type=F32)
    gain_row = 1.0 - step_size * (2.0 * diag_ref[...] + penalty)
    for l in range(leaves):
        goal = small[0:sections, leaves + l : leaves + l + 1]
        here = nat[leaf_rows(l), :]
        fixed = step_size * (cost_v[l].astype(F32) + dual_v[l] - penalty * here - coupling * goal)
        fixed_nat[leaf_rows(l), :] = fixed
        nat[leaf_rows(l), :] = (
            gain_row * here - step_size * image[l * sections : (l + 1) * sections, :] - fixed
        )
    for b in range(lane_blocks):
        pre[:, lanes(b)] = nat[lanes(b), :].T

    def update(step):
        term = head_term(step - 1)
        part = jnp.zeros((8, rows), F32)
        for b in range(nodes // 64):
            some = slice(b * 64, (b + 1) * 64)
            new = jnp.clip(pre[some, :] - term, -power_limit, power_limit)
            xt[some, :] = new
            part = part + jnp.sum(new.reshape(8, 8, rows), axis=0)
        head_send[step] = jnp.sum(part, axis=0, keepdims=True)
        send_heads(step)

    def advance(step, carry):
        update(step)
        window()
        return carry

    update(1)
    q_t[...] = q_m[...].T
    for b in range(lane_blocks):
        fixed_t[:, lanes(b)] = fixed_nat[lanes(b), :].T
    gain_t[...] = jnp.broadcast_to(gain_row, (LANES, nodes)).T
    window()

    advance(2, 0)

    wide = (sections, LANES)

    def leaf_id(l):
        return jnp.broadcast_to(small[0:sections, l : l + 1], wide)

    ids = [leaf_id(l) for l in range(leaves)]
    run_w = [jnp.full(wide, weight_ref[0], F32)]
    for l in range(1, leaves):
        link = (ids[l] == ids[l - 1]).astype(F32)
        same[l] = link
        run_w.append(link * run_w[-1] + weight_ref[l])
    own_w = run_w[leaves - 1]
    total_w[leaves - 1] = own_w
    for l in range(leaves - 2, -1, -1):
        own_w = jnp.where(ids[l] == ids[l + 1], own_w, run_w[l])
        total_w[l] = own_w
    column = lax.broadcasted_iota(jnp.int32, wide, 1)
    note_send[...] = jnp.where(
        column == 0,
        run_w[leaves - 1],
        jnp.where(column == 1, ids[leaves - 1], jnp.where(column == 2, own_w, ids[0])),
    )
    for k in range(1, ns):
        pltpu.make_async_remote_copy(
            src_ref=note_send,
            dst_ref=note_recv.at[k - 1],
            send_sem=note_ssem,
            recv_sem=note_rsem,
            device_id=(mf, lax.rem(ms + k, ns)),
            device_id_type=MESH,
        ).start()

    lax.fori_loop(3, 5, advance, 0)

    pltpu.make_async_copy(note_recv, note_recv, note_rsem).wait()
    pltpu.make_async_copy(note_recv, note_recv, note_ssem).wait()
    first_id = leaf_id(0)
    last_id = leaf_id(leaves - 1)
    start = (ms * leaves).astype(F32)
    goes_back = (first_id < start).astype(F32)
    spans = (last_id < start).astype(F32)
    left_w = jnp.zeros(wide, F32)
    right_w = jnp.zeros(wide, F32)
    for k in range(1, ns):
        note = note_recv[k - 1]
        earlier = jnp.where(ms >= k, 1.0, 0.0)
        left_w += earlier * jnp.where(note[:, 1:2] == first_id, note[:, 0:1], 0.0)
        right_w += (1.0 - earlier) * jnp.where(note[:, 3:4] == last_id, note[:, 2:3], 0.0)
    packed = jnp.zeros(wide, F32)
    for l in range(leaves):
        own_id = leaf_id(l)
        in_first = (own_id == first_id).astype(F32)
        in_last = (own_id == last_id).astype(F32)
        scale = 1.0 / (total_w[l] + in_first * left_w + in_last * right_w)
        total_w[l] = scale
        packed = jnp.where(column == l, in_first * goes_back * scale, packed)
        packed = jnp.where(column == leaves + l, in_last * scale, packed)
    packed_ref[2 * node_blocks] = packed

    lax.fori_loop(5, PROX_ITERS, advance, 0)

    for b in range(lane_blocks):
        nat[lanes(b), :] = pre[:, lanes(b)].T
    term = head_term(PROX_ITERS - 1)
    for b in range(lane_blocks):
        head_col[lanes(b), :] = jnp.broadcast_to(term[:, b * LANES : (b + 1) * LANES], (LANES, LANES)).T

    half = node_blocks // 2

    def up_copy(p):
        some = pl.ds(p * half, half)
        return pltpu.make_async_remote_copy(
            src_ref=up_send.at[some], dst_ref=up_recv.at[some],
            send_sem=up_ssem.at[p], recv_sem=up_rsem.at[p],
            device_id=(mf, lax.rem(ms + 1, ns)), device_id_type=MESH,
        )

    def down_copy(p):
        some = pl.ds(p * half, half)
        return pltpu.make_async_remote_copy(
            src_ref=down_send.at[some], dst_ref=down_recv.at[some],
            send_sem=down_ssem.at[p], recv_sem=down_rsem.at[p],
            device_id=(mf, lax.rem(ms + ns - 1, ns)), device_id_type=MESH,
        )

    at_bottom, at_top = ms == 0, ms == ns - 1
    for c in range(node_blocks):
        run = None
        for l in range(leaves):
            x = jnp.clip(nat[leaf_rows(l), lanes(c)] - head_col[leaf_rows(l), :], -power_limit, power_limit)
            x_out[l, :, lanes(c)] = x
            weighted = weight_ref[l] * x
            if l == 0:
                run = weighted
                opening = weighted
                in_first = goes_back
            else:
                run = weighted + same[l] * run
                in_first = in_first * same[l]
                opening = opening + in_first * weighted
            own_out[l, :, lanes(c)] = run
        opening = opening * goes_back
        tail[c] = run
        front[c] = opening

        @pl.when(at_bottom)
        def _():
            up_send[c] = run
            if c % half == half - 1:
                up_copy(c // half).start()

        @pl.when(at_top)
        def _():
            down_send[c] = opening
            if c % half == half - 1:
                down_copy(c // half).start()

    for c in range(node_blocks):
        run = tail[c]
        for l in range(leaves - 1, -1, -1):
            if l < leaves - 1:
                run = jnp.where(same[l + 1] > 0.5, run, own_out[l, :, lanes(c)])
            own_out[l, :, lanes(c)] = run * total_w[l]

    def upward():
        for p in range(2):
            up_copy(p).wait_recv()

            @pl.when(jnp.logical_not(at_top))
            def _():
                for c in range(p * half, (p + 1) * half):
                    up_send[c] = tail[c] + spans * up_recv[c]
                up_copy(p).start()

    def downward():
        for p in range(2):
            down_copy(p).wait_recv()

            @pl.when(jnp.logical_not(at_bottom))
            def _():
                for c in range(p * half, (p + 1) * half):
                    down_send[c] = front[c] + spans * down_recv[c]
                down_copy(p).start()

    low = ms < ns // 2

    @pl.when(at_bottom)
    def _():
        up_recv[...] = jnp.zeros_like(up_recv)

    @pl.when(at_top)
    def _():
        down_recv[...] = jnp.zeros_like(down_recv)

    @pl.when(jnp.logical_and(low, jnp.logical_not(at_bottom)))
    def _():
        upward()

    @pl.when(jnp.logical_not(at_top))
    def _():
        downward()

    @pl.when(jnp.logical_not(low))
    def _():
        upward()

    for c in range(node_blocks):
        packed_ref[c] = up_recv[c]
        packed_ref[node_blocks + c] = down_recv[c]
    for p in range(2):

        @pl.when(jnp.logical_not(at_top))
        def _():
            up_copy(p).wait_send()

        @pl.when(jnp.logical_not(at_bottom))
        def _():
            down_copy(p).wait_send()

    for step in range(PROX_ITERS):
        pltpu.make_async_copy(head_recv.at[step], head_recv.at[step], head_ssem.at[step]).wait()


def finish(x_ref, own_ref, dual_ref, packed_ref, xout_hbm, avg_hbm, newdual_hbm, avg_v, new_v, coef, out_sem):
    leaves, sections, nodes = x_ref.shape
    node_blocks = nodes // LANES
    group = 4

    def store(first, i, src, dst):
        some = pl.ds(first, group)
        return pltpu.make_async_copy(src.at[some], dst.at[some], out_sem.at[3 * (first // group) + i])

    stores = [store(l, 0, x_ref, xout_hbm) for l in range(0, leaves, group)]
    for copy in stores:
        copy.start()
    packed = packed_ref[2 * node_blocks]
    for i in range(2 * leaves):
        coef[i] = jnp.broadcast_to(packed[:, i : i + 1], (sections, LANES))
    for l in range(leaves):
        for c in range(node_blocks):
            some = pl.ds(c * LANES, LANES)
            average = (
                own_ref[l, :, some]
                + coef[l] * packed_ref[c]
                + coef[leaves + l] * packed_ref[node_blocks + c]
            )
            avg_v[l, :, some] = average
            new_v[l, :, some] = dual_ref[l, :, some] + penalty * (x_ref[l, :, some] - average)
        if l % group == group - 1:
            first = l - group + 1
            for copy in (store(first, 1, avg_v, avg_hbm), store(first, 2, new_v, newdual_hbm)):
                copy.start()
                stores.append(copy)
    for copy in stores:
        copy.wait()


def local(nf, ns, anchor, cost_lin, dual, target, leaf_weight, q_mat, diag_gain, block_mask, ancestor):
    leaves, sections, nodes = anchor.shape
    rows = leaves * sections
    blocks = nodes // LANES
    vmem, smem = pltpu.VMEM, pltpu.SMEM
    dma = pltpu.SemaphoreType.DMA
    cube = (leaves, sections, nodes)
    coef = (leaves, sections, LANES)
    piece = (blocks, sections, LANES)
    out = jax.ShapeDtypeStruct(cube, F32)
    hbm = pl.BlockSpec(memory_space=pltpu.HBM)
    far = pl.BlockSpec(memory_space=pl.ANY)
    near = pl.BlockSpec(memory_space=vmem)
    packed = jax.ShapeDtypeStruct((2 * blocks + 1, sections, LANES), F32)
    limit = 24 * 1024 * 1024
    state, own, parts = pl.pallas_call(
        functools.partial(kernel, nf, ns),
        out_shape=(out, out, packed),
        in_specs=[hbm] * 9,
        out_specs=(near, near, near),
        scratch_shapes=[
            vmem((leaves, sections), F32), smem((leaves,), F32), vmem((1, nodes), F32),
            smem(block_mask.shape, jnp.int32), vmem((leaves, sections), jnp.int32),
            vmem(cube, BF16), vmem(cube, BF16), vmem(cube, F32), vmem((nodes, nodes), BF16),
            vmem((nodes, nodes), BF16), vmem((rows, nodes), BF16), vmem((rows, nodes), F32), vmem((rows, nodes), F32),
            vmem((nodes, rows), F32), vmem((nodes, rows), F32), vmem((nodes, rows), F32),
            vmem((nodes, nodes), BF16), vmem((nodes, LANES), F32), vmem((rows, LANES), F32),
            vmem((LANES, LANES), F32),
            vmem(coef, F32), vmem(coef, F32),
            vmem((PROX_ITERS, 1, rows), F32), vmem((PROX_ITERS, nf - 1, 1, rows), F32),
            vmem((sections, LANES), F32), vmem((ns - 1, sections, LANES), F32),
            vmem(piece, F32), vmem(piece, F32), vmem(piece, F32), vmem(piece, F32),
            vmem(piece, F32), vmem(piece, F32),
            dma((9,)), dma((PROX_ITERS,)), dma((PROX_ITERS,)), dma, dma,
            dma((2,)), dma((2,)), dma((2,)), dma((2,)),
        ],
        compiler_params=pltpu.CompilerParams(
            collective_id=0, has_side_effects=True, vmem_limit_bytes=limit
        ),
        cost_estimate=pl.CostEstimate(
            flops=2 * PROX_ITERS * rows * nodes * nodes, bytes_accessed=12 * rows * nodes, transcendentals=0
        ),
    )(
        *(
            pltpu.with_memory_space_constraint(array, pltpu.HBM)
            for array in (
                anchor, cost_lin, dual, q_mat, target, leaf_weight, diag_gain.reshape(1, nodes), block_mask,
                ancestor.T,
            )
        )
    )
    return pl.pallas_call(
        finish,
        out_shape=(out, out, out),
        in_specs=[near, near, near, near],
        out_specs=(far, far, far),
        scratch_shapes=[
            vmem(cube, F32), vmem(cube, F32), vmem((2 * leaves, sections, LANES), F32), dma((3 * leaves // 4,)),
        ],
        compiler_params=pltpu.CompilerParams(vmem_limit_bytes=limit),
        cost_estimate=pl.CostEstimate(flops=8 * rows * nodes, bytes_accessed=24 * rows * nodes, transcendentals=0),
    )(state, own, dual, parts)


def solution(mesh):
    return jax.shard_map(
        functools.partial(local, mesh.shape["feeder"], mesh.shape["scen"]),
        mesh=mesh,
        in_specs=(
            P("scen", None, "feeder"),
            P("scen", None, "feeder"),
            P("scen", None, "feeder"),
            P("scen", None),
            P("scen"),
            P("feeder", None),
            P("feeder"),
            P("feeder", None, None),
            P(None, "scen"),
        ),
        out_specs=(P("scen", None, "feeder"), P("scen", None, "feeder"), P("scen", None, "feeder")),
        check_vma=False,
    )
```
